128 devices in a mesh: leaf: 32 (over z, y, core), sub: 4 (over x).
Axes of the slice: x: 4, y: 4, z: 4, core: 2. Of those that a mesh axis runs over, the one named last changes fastest.
Arguments:
- density: float32 [4, 2048, 128], P(None, ('leaf', 'sub')), may hold values from -6 to 6
- centres: float32 [3, 2048, 128], P(None, ('leaf', 'sub')), may hold values from 0 to 1
- normal: float32 [3, 2048, 128], P(None, ('leaf', 'sub')), may hold values from -0.10206208 to 0.10206208
- to_multipole: bfloat16 [2048, 152, 128], P(('leaf', 'sub')), may hold values from -0.5 to 0.5
- to_panels: bfloat16 [2048, 128, 152], P(('leaf', 'sub')), may hold values from -0.5 to 0.5
- m2m_ops: bfloat16 [8, 152, 152], replicated, may hold values from -0.5 to 0.5
- l2l_ops: bfloat16 [8, 152, 152], replicated, may hold values from -0.5 to 0.5
- m2l_ops: bfloat16 [316, 152, 152], replicated, may hold values from -0.078125 to 0.078125
- near_index: int32 [2048, 27], P(('leaf', 'sub')), may hold values from 0 to 23
- near_count: int32 [2048], P(('leaf', 'sub')), may hold values from 1 to 27
- send_box: int32 [128, 128, 2], P(('leaf', 'sub')), may hold values from 0 to 15
- send_count: int32 [128, 128], P(('leaf', 'sub')), may hold values from 0 to 2, as said below
- far_slot: int32 [2048, 64], P(('leaf', 'sub')), may hold values from 0 to 255, as said below
- far_op: int32 [2048, 64], P(('leaf', 'sub')), may hold values from 0 to 315
- far_count: int32 [2048], P(('leaf', 'sub')), may hold values from 1 to 64
- parent_of: int32 [32, 64], P('leaf', 'sub'), may hold values from 0 to 15, never falling along the last dimension, each value on 1 to 8 neighbouring positions
- octant: int32 [32, 64], P('leaf', 'sub'), may hold values from 0 to 7
- top_src: int32 [512, 32], P('leaf'), may hold values from 0 to 511
- top_op: int32 [512, 32], P('leaf'), may hold values from 0 to 315
- top_count: int32 [512], P('leaf'), may hold values from 1 to 32
Outputs:
- potential: float32 [4, 2048, 128], P(None, ('leaf', 'sub'))
The draws below stay inside these ranges and needn't reach their ends.
Inputs may be any that keep to these rules, and one draw needn't show every extreme that they name: `parent_of`: within each row, parent numbers never fall, each of 0 to 15 appears, at most 8 times, one exactly 8 times. `send_count`: every device receives at least one valid slot; in every draw one receiving device gets 2 valid slots from every sender. `far_slot`: each entry of a leaf on device d is s * 2 + j with j < send_count[s, d].
All inputs are finite; a program needn't handle non-finite values.
Results may differ from the reference program's by a relative error of at most 0.002.
Values may be sent and summed in bfloat16 or wider, within the bound.
No kernel may reach another device: no remote copies, remote signals or barrier semaphores. Data moves between devices by JAX's collectives and lax.ppermute only.
A program may use at most 128 MiB of HBM per device.

```python
import math
import jax
import jax.numpy as jnp
import numpy as np
from jax import lax

PANELS = 128
EQUIV = 152
RHS = 4
OPS = 316
NEAR_MAX = 27
FAR_MAX = 64
PFAR_MAX = 32
RIM = 4
LEAF_DEV = 16
PAR_DEV = 16
SLOTS = 2
PEERS = 128
LEAVES = 2048
PARENTS = 512
N_LEAF = 32
N_SUB = 4


def counts_table(key):
    key = jax.random.fold_in(key, 11)
    first_key, second_key = jax.random.split(key)
    count_table = jax.random.randint(first_key, (PEERS, PEERS), 0, SLOTS + 1)
    full_column = jax.random.randint(second_key, (), 0, PEERS)
    column = jnp.arange(PEERS)[None, :]
    sender_ids = jnp.arange(PEERS)[:, None]
    count_table = jnp.where(column == full_column, SLOTS, count_table)
    beside = (column + 1) % PEERS == sender_ids
    count_table = jnp.where(beside, jnp.maximum(count_table, 1), count_table)
    return count_table.astype(jnp.int32)


def draw_send_count(key, part):
    return counts_table(key)


def draw_far_slot(key, part):
    count_table = counts_table(key)
    key = jax.random.fold_in(key, 5)
    slot_ids = jnp.arange(SLOTS)

    def per_receiver(column, sub_key):
        valid_mask = (slot_ids[None, :] < column[:, None]).reshape(-1).astype(jnp.int32)
        running = jnp.cumsum(valid_mask)
        picked = jax.random.randint(sub_key, (LEAF_DEV * FAR_MAX,), 0, running[-1])
        return jnp.searchsorted(running, picked, side='right').astype(jnp.int32)
    receiver_keys = jax.random.split(key, PEERS)
    result = jax.vmap(per_receiver)(count_table.T, receiver_keys)
    return result.reshape(LEAVES, FAR_MAX)


def touch_ends(drawn, own_key, smallest, top_value):
    longest = drawn.shape.index(max(drawn.shape))
    spots = []
    for shift in (0, 1):
        where = [jax.random.randint(jax.random.fold_in(own_key, axis), (), 0, length) for axis, length in enumerate(drawn.shape)]
        where[longest] = (where[longest] + shift) % drawn.shape[longest]
        spots.append(tuple(where))
    return drawn.at[spots[0]].set(smallest).at[spots[1]].set(top_value)


def levels(own_key, shape, cuts, smallest, largest):
    def one(position, parts):
        draws = jax.random.uniform(jax.random.fold_in(jax.random.fold_in(own_key, 6), position), (parts,), jnp.float32, smallest / len(cuts), largest / len(cuts))
        return jnp.repeat(jnp.exp(draws), shape[position] // parts).reshape((-1,) + (1,) * (len(shape) - position - 1))

    level = one(*cuts[0])
    for cut in cuts[1:]:
        level = level * one(*cut)
    return level


def split_up(number_of, total, most, slope):
    weights = [(1 << 20) // math.isqrt(rank ** slope) + 1 for rank in range(2, number_of + 1)]
    rest, given = total - most - (number_of - 1), [1] * (number_of - 1)
    while rest > 0:
        free = [i for i in range(number_of - 1) if given[i] < most]
        whole, remaining = sum([weights[i] for i in free]), rest
        for i in free:
            extra = min(most - given[i], max(1, remaining * weights[i] // whole), rest)
            given[i] = given[i] + extra
            rest = rest - extra
    return np.array([most] + given)


def ragged(own_key, amount, total, bound, skew):
    if amount == 2:
        one = jax.random.randint(own_key, (), max(1, total - bound), min(bound, total - 1) + 1)
        return jnp.stack([one, total - one])
    lengths = jnp.asarray(split_up(amount, total, bound, skew), jnp.int32)
    pairs = (amount - 1) // 2
    giver, taker = lengths[1:1 + 2 * pairs:2], lengths[2:2 + 2 * pairs:2]
    slack = jnp.minimum(giver - 1, bound - taker)
    passed = jax.random.randint(jax.random.fold_in(own_key, 1), (pairs,), 0, 1 << 20) % (slack + 1)
    lengths = lengths.at[1:1 + 2 * pairs:2].set(giver - passed).at[2:2 + 2 * pairs:2].set(taker + passed)
    return lengths[jax.random.permutation(jax.random.fold_in(own_key, 2), amount)]


def scatter_about(stream_key, shape, scale, bound, shards=(), kind=jnp.bfloat16):
    values = scale * jax.random.normal(stream_key, shape, jnp.float32)
    if shards:
        values = values * levels(stream_key, shape, shards, -0.22, 0.18)
    return jnp.clip(values, -bound, bound).astype(kind)


def setup_inputs(seed: int = 0) -> dict:
    keys = jax.random.split(jax.random.key(seed), 21)
    return {
        "density": scatter_about(keys[0], (RHS, LEAVES, PANELS), 1.0, 6.0, ((1, 128),), jnp.float32),
        "centres": jnp.clip(1.0 * jax.random.uniform(keys[1], (3, LEAVES, PANELS), jnp.float32) ** levels(keys[1], (3, LEAVES, PANELS), ((1, 128),), -0.2, 0.2), 0.0, 1.0),
        "normal": scatter_about(keys[2], (3, LEAVES, PANELS), (1.0 / (NEAR_MAX * PANELS) ** 0.5), 0.10206208, ((1, 128),), jnp.float32),
        "to_multipole": scatter_about(keys[3], (LEAVES, EQUIV, PANELS), PANELS ** -0.5, 0.5, ((0, 128),)),
        "to_panels": scatter_about(keys[4], (LEAVES, PANELS, EQUIV), EQUIV ** -0.5, 0.5, ((0, 128),)),
        "m2m_ops": scatter_about(keys[5], (8, EQUIV, EQUIV), EQUIV ** -0.5, 0.5),
        "l2l_ops": scatter_about(keys[6], (8, EQUIV, EQUIV), EQUIV ** -0.5, 0.5),
        "m2l_ops": scatter_about(keys[7], (OPS, EQUIV, EQUIV), (EQUIV * FAR_MAX // 2) ** -0.5, 0.078125),
        "near_index": touch_ends(jax.random.randint(keys[8], (LEAVES, NEAR_MAX), 0, LEAF_DEV + 2 * RIM), jax.random.fold_in(keys[8], 1), 0, (LEAF_DEV + 2 * RIM) - 1).astype(jnp.int32),
        "near_count": touch_ends(jax.random.randint(keys[9], (LEAVES,), 1, NEAR_MAX + 1), jax.random.fold_in(keys[9], 1), 1, NEAR_MAX).astype(jnp.int32),
        "send_box": touch_ends(jax.random.randint(keys[10], (PEERS, PEERS, SLOTS), 0, LEAF_DEV), jax.random.fold_in(keys[10], 1), 0, LEAF_DEV - 1).astype(jnp.int32),
        "send_count": draw_send_count(jax.random.fold_in(keys[20], 71), 0),
        "far_slot": draw_far_slot(jax.random.fold_in(keys[20], 71), 0),
        "far_op": touch_ends(jax.random.randint(keys[13], (LEAVES, FAR_MAX), 0, OPS), jax.random.fold_in(keys[13], 1), 0, OPS - 1).astype(jnp.int32),
        "far_count": touch_ends(jax.random.randint(keys[14], (LEAVES,), 1, FAR_MAX + 1), jax.random.fold_in(keys[14], 1), 1, FAR_MAX).astype(jnp.int32),
        "parent_of": jax.vmap(lambda own: jnp.searchsorted(jnp.cumsum(ragged(own, PAR_DEV, N_SUB * LEAF_DEV, 8, 1)), jnp.arange(N_SUB * LEAF_DEV), side="right"))(jax.random.split(keys[15], N_LEAF)).reshape((N_LEAF, N_SUB * LEAF_DEV)).astype(jnp.int32),
        "octant": touch_ends(jax.random.randint(keys[16], (N_LEAF, N_SUB * LEAF_DEV), 0, 8), jax.random.fold_in(keys[16], 1), 0, 7).astype(jnp.int32),
        "top_src": touch_ends(jax.random.randint(keys[17], (PARENTS, PFAR_MAX), 0, PARENTS), jax.random.fold_in(keys[17], 1), 0, PARENTS - 1).astype(jnp.int32),
        "top_op": touch_ends(jax.random.randint(keys[18], (PARENTS, PFAR_MAX), 0, OPS), jax.random.fold_in(keys[18], 1), 0, OPS - 1).astype(jnp.int32),
        "top_count": touch_ends(jax.random.randint(keys[19], (PARENTS,), 1, PFAR_MAX + 1), jax.random.fold_in(keys[19], 1), 1, PFAR_MAX).astype(jnp.int32),
    }


core_square = 0.01

def near_leaves(targets, sources, alive_mask):
    radius_sq = core_square
    projection = 0.0
    for axis_id in range(3):
        offset = targets[axis_id][:, :, None, None] - sources[axis_id][:, None, :, :]
        radius_sq = radius_sq + offset * offset
        projection = projection + sources[3 + axis_id][:, None, :, :] * offset
    kernel = projection / (radius_sq * jnp.sqrt(radius_sq))
    weights = sources[6:] * alive_mask[None, :, :, None]
    return jnp.einsum('btks,rbks->brt', kernel, weights, precision=lax.Precision.HIGHEST)

def near_field(density, centres, normal, near_index, near_count):
    stacked = jnp.concatenate([centres, normal, density], 0)
    border = jnp.zeros((stacked.shape[0], RIM, PANELS), jnp.float32)
    padded = jnp.concatenate([border, stacked, border], 1)
    leaf_ids = jnp.arange(LEAVES, dtype=jnp.int32)
    row_ids = (leaf_ids // LEAF_DEV * LEAF_DEV)[:, None] + near_index
    live_mask = (jnp.arange(NEAR_MAX, dtype=jnp.int32)[None, :] < near_count[:, None]).astype(jnp.float32)

    def one_block(first_row):
        targets = lax.dynamic_slice_in_dim(centres, first_row, 4, 1)
        picked = lax.dynamic_slice_in_dim(row_ids, first_row, 4, 0)
        alive_mask = lax.dynamic_slice_in_dim(live_mask, first_row, 4, 0)
        return near_leaves(targets, padded[:, picked], alive_mask)
    starts = jnp.arange(0, LEAVES, 4, dtype=jnp.int32)
    return lax.map(one_block, starts).reshape(LEAVES, RHS, PANELS)

def translate(box_table, tables, row_ids, kind_ids, live_mask):
    row_count = row_ids.shape[0]
    block_size = math.gcd(8, row_count)

    def one_block(first_row):
        picked = lax.dynamic_slice_in_dim(row_ids, first_row, block_size, 0)
        chosen = lax.dynamic_slice_in_dim(kind_ids, first_row, block_size, 0)
        alive_mask = lax.dynamic_slice_in_dim(live_mask, first_row, block_size, 0)
        sources = box_table[picked].astype(jnp.float32) * alive_mask[:, :, None, None]
        matrices = tables[chosen].astype(jnp.float32)
        return jnp.einsum('bkef,bkrf->bre', matrices, sources)
    starts = jnp.arange(0, row_count, block_size, dtype=jnp.int32)
    return lax.map(one_block, starts).reshape(row_count, RHS, EQUIV)

def by_octant(tables, octants, vectors):
    summed = jnp.zeros(vectors.shape, jnp.float32)
    widened = vectors.astype(jnp.float32)
    for octant_id in range(8):
        rotated = jnp.einsum('ef,nrf->nre', tables[octant_id].astype(jnp.float32), widened)
        summed = summed + jnp.where((octants == octant_id)[:, None, None], rotated, 0.0)
    return summed

def reference(density, centres, normal, to_multipole, to_panels, m2m_ops, l2l_ops, m2l_ops, near_index, near_count, send_box, send_count, far_slot, far_op, far_count, parent_of, octant, top_src, top_op, top_count):
    near_part = near_field(density, centres, normal, near_index, near_count)
    density_low = density.astype(jnp.bfloat16)
    multipole = jnp.einsum('nep,rnp->nre', to_multipole.astype(jnp.float32), density_low.astype(jnp.float32)).astype(jnp.bfloat16)
    octants = octant.reshape(-1)
    leaf_ids = jnp.arange(LEAVES, dtype=jnp.int32)
    parent_ids = leaf_ids // (N_SUB * LEAF_DEV) * PAR_DEV + parent_of.reshape(-1)
    children = by_octant(m2m_ops, octants, multipole)
    parent_mult = jax.ops.segment_sum(children, parent_ids, num_segments=PARENTS).astype(jnp.bfloat16)
    top_live = (jnp.arange(PFAR_MAX, dtype=jnp.int32)[None, :] < top_count[:, None]).astype(jnp.float32)
    parent_local = translate(parent_mult, m2l_ops, top_src, top_op, top_live).astype(jnp.bfloat16)
    downward = by_octant(l2l_ops, octants, parent_local[parent_ids])
    receiver = (leaf_ids // LEAF_DEV)[:, None]
    sender = far_slot // SLOTS
    place = far_slot % SLOTS
    box_ids = sender * LEAF_DEV + send_box[sender, receiver, place]
    far_live = (jnp.arange(FAR_MAX, dtype=jnp.int32)[None, :] < far_count[:, None]) & (place < send_count[sender, receiver])
    far_part = translate(multipole, m2l_ops, box_ids, far_op, far_live.astype(jnp.float32))
    local_exp = (downward + far_part).astype(jnp.bfloat16)
    potential = jnp.einsum('npe,nre->rnp', to_panels.astype(jnp.float32), local_exp.astype(jnp.float32))
    return potential + jnp.transpose(near_part, (1, 0, 2))
```

```python
import jax
import jax.numpy as jnp
from jax import lax
from jax.experimental import pallas as pl
from jax.experimental.pallas import tpu as pltpu
from jax.sharding import PartitionSpec as P

f32 = jnp.float32
bf16 = jnp.bfloat16
i32 = jnp.int32

RIM = 4
LEAF = 16
RHS = 4
ROWS = RHS * LEAF
EQ = 152
EQP = 160
OPSP = 384
PAN = 128
BOX = 640
SLOT = 8
EPS = 0.01
FB = 8
MIB = 1 << 20

VM = pl.BlockSpec(memory_space=pltpu.VMEM)
SM = pl.BlockSpec(memory_space=pltpu.SMEM)


def nt(a, b, **kw):
    return lax.dot_general(a, b, (((1,), (1,)), ((), ())), preferred_element_type=f32, **kw)


def nn(a, b, **kw):
    return lax.dot_general(a, b, (((1,), (0,)), ((), ())), preferred_element_type=f32, **kw)


def iota(shape, dim):
    return lax.broadcasted_iota(i32, shape, dim)


def upward_kernel(par, octs, dens, cen, nrm, tm, m2m, mult_out, part_out, low_out, high_out):
    d = dens[...].astype(bf16)
    leaf_row = iota((ROWS, EQ), 0) % LEAF
    mult = jnp.zeros((ROWS, EQ), f32)
    for n in range(LEAF):
        mult = jnp.where(leaf_row == n, nt(d, tm[n]), mult)
    mb = mult.astype(bf16)
    mult_out[...] = mb
    child = jnp.zeros((ROWS, EQ), f32)
    for n in range(LEAF):
        child = jnp.where(leaf_row == n, nt(mb, m2m[octs[0, n]]), child)
    row = iota((ROWS, ROWS), 0)
    lane = iota((ROWS, ROWS), 1)
    parent = jnp.zeros((ROWS, ROWS), i32)
    for n in range(LEAF):
        parent = jnp.where(lane % LEAF == n, par[0, n], parent)
    box = (row // 16) * 4 + row % 4
    hit = (parent == box) & ((row // 4) % 4 == lane // LEAF)
    part_out[...] = nn(hit.astype(f32), child, precision=lax.Precision.HIGHEST)
    for a in range(3):
        high_out[4 * a : 4 * a + 4, :] = cen[a, :RIM, :]
        low_out[4 * a : 4 * a + 4, :] = cen[a, LEAF - RIM :, :]
        high_out[12 + 4 * a : 16 + 4 * a, :] = nrm[a, :RIM, :]
        low_out[12 + 4 * a : 16 + 4 * a, :] = nrm[a, LEAF - RIM :, :]
    for r in range(RHS):
        high_out[24 + 4 * r : 28 + 4 * r, :] = dens[LEAF * r : LEAF * r + RIM, :]
        low_out[24 + 4 * r : 28 + 4 * r, :] = dens[LEAF * (r + 1) - RIM : LEAF * (r + 1), :]


def upward(par, octs, dens, cen, nrm, tm, m2m):
    return pl.pallas_call(
        upward_kernel,
        in_specs=[SM, SM, VM, VM, VM, VM, VM],
        out_specs=[VM] * 4,
        out_shape=[
            jax.ShapeDtypeStruct((ROWS, EQ), bf16),
            jax.ShapeDtypeStruct((ROWS, EQ), f32),
            jax.ShapeDtypeStruct((40, PAN), f32),
            jax.ShapeDtypeStruct((40, PAN), f32),
        ],
        compiler_params=pltpu.CompilerParams(vmem_limit_bytes=16 * MIB),
        name="upward",
    )(par, octs, dens, cen, nrm, tm, m2m)


def pack_kernel(ids, mult, pieces, out):
    row = iota((EQ, BOX), 0)
    lane = iota((EQ, BOX), 1)
    own = pieces[0:16, :]
    for s in range(1, 4):
        own = own + pieces[16 * s : 16 * s + 16, :]
    own = own.astype(bf16).astype(f32)
    mf = mult[...].astype(f32)
    table = jnp.zeros((24, BOX), f32)
    for r in range(RHS):
        both = jnp.concatenate(
            [mf[16 * r : 16 * r + 16], own[4 * r : 4 * r + 4], jnp.zeros((4, EQ), f32)], 0
        )
        place = (lane == row + EQ * r).astype(f32).astype(bf16)
        table = table + nn(both.astype(bf16), place)
    hot = (ids[...] == iota((128 * SLOT, 24), 1)).astype(f32).astype(bf16)
    out[...] = nn(hot, table.astype(bf16)).astype(bf16)


def pack(ids, mult, pieces):
    return pl.pallas_call(
        pack_kernel,
        in_specs=[VM] * 3,
        out_specs=VM,
        out_shape=jax.ShapeDtypeStruct((128 * SLOT, BOX), bf16),
        compiler_params=pltpu.CompilerParams(vmem_limit_bytes=24 * MIB),
        name="pack",
    )(ids, mult, pieces)


def reorder_kernel(src, out):
    e0 = pl.program_id(0) * 16
    ops = src.shape[2]
    row = iota((256, 256), 0)
    lane = iota((256, 256), 1)
    perm = (lane == (row % 16) * 16 + row // 16).astype(f32).astype(bf16)
    e_row = e0 + iota((16, 16, ops), 0)
    for j in range(10):
        block = src[:, 16 * j : 16 * j + 16, :]
        live = e_row < EQ
        if j == 9:
            live = live & (iota((16, 16, ops), 1) < EQ - 144)
        block = jnp.where(live, block, jnp.zeros((), bf16)).reshape(256, ops)
        moved = nn(perm, block).astype(bf16)
        moved = jnp.concatenate([moved, jnp.zeros((256, OPSP - ops), bf16)], 1)
        moved = moved.reshape(16, 16, OPSP)
        if j == 9:
            out[144:EQ] = moved[: EQ - 144]
        else:
            out[16 * j : 16 * j + 16] = moved


def reorder(tables):
    ops = tables.shape[2]
    return pl.pallas_call(
        reorder_kernel,
        grid=(10,),
        in_specs=[pl.BlockSpec((16, EQP, ops), lambda i: (i, 0, 0))],
        out_specs=pl.BlockSpec((EQ, 16, OPSP), lambda i: (0, i, 0)),
        out_shape=jax.ShapeDtypeStruct((EQ, EQP, OPSP), bf16),
        compiler_params=pltpu.CompilerParams(vmem_limit_bytes=32 * MIB),
        cost_estimate=pl.CostEstimate(
            flops=2 * 100 * 256 * 256 * 384, bytes_accessed=37_000_000, transcendentals=0
        ),
        name="reorder",
    )(tables)


SRC = LEAF + 2 * RIM
FEAT = 48
ORDERS = ((0, 0), (0, 1), (1, 0), (0, 2), (1, 1), (2, 0))


def three(x):
    a = x.astype(bf16).astype(f32)
    b = (x - a).astype(bf16).astype(f32)
    c = (x - a - b).astype(bf16).astype(f32)
    return a, b, c


def near_kernel(index, count, cen, nrm, dens, low, high, out, raw, fsrc, ftar, fs, dtab):
    for q in range(10):
        raw[q, 0:RIM, :] = low[4 * q : 4 * q + 4, :]
        raw[q, RIM + LEAF : SRC, :] = high[4 * q : 4 * q + 4, :]
        if q < 3:
            body = cen[q]
        elif q < 6:
            body = nrm[q - 3]
        else:
            body = dens[LEAF * (q - 6) : LEAF * (q - 5), :]
        raw[q, RIM : RIM + LEAF, :] = body
    xs = [raw[a] - 0.5 for a in range(3)]
    ns = [raw[3 + a] for a in range(3)]
    xt = [cen[a] - 0.5 for a in range(3)]
    xs3 = [three(v) for v in xs]
    ns3 = [three(v) for v in ns]
    xt3 = [three(v) for v in xt]
    ss = three(xs[0] * xs[0] + xs[1] * xs[1] + xs[2] * xs[2] + EPS)
    sn = three(xs[0] * ns[0] + xs[1] * ns[1] + xs[2] * ns[2])
    tt = three(xt[0] * xt[0] + xt[1] * xt[1] + xt[2] * xt[2])
    one_s = jnp.ones((SRC, PAN), f32)
    zero_s = jnp.zeros((SRC, PAN), f32)
    one = jnp.ones((LEAF, PAN), f32)
    zero = jnp.zeros((LEAF, PAN), f32)
    feats = []
    for a in range(3):
        for i, j in ORDERS:
            feats.append((xs3[a][i], -2.0 * xt3[a][j], zero))
            feats.append((ns3[a][i], zero, xt3[a][j]))
    for i in range(3):
        feats.append((ss[i], one, zero))
        feats.append((sn[i], zero, -one))
        feats.append((one_s, tt[i], zero))
    while len(feats) < FEAT:
        feats.append((zero_s, zero, zero))
    for k, (s, t1, t2) in enumerate(feats):
        fsrc[k * SRC : (k + 1) * SRC, :] = s
        ftar[0, k * LEAF : (k + 1) * LEAF, :] = t1
        ftar[1, k * LEAF : (k + 1) * LEAF, :] = t2
    for r in range(RHS):
        d = raw[6 + r]
        hi = d.astype(bf16).astype(f32)
        dtab[pl.ds(r, SRC, stride=8), :] = hi
        dtab[pl.ds(RHS + r, SRC, stride=8), :] = (d - hi).astype(bf16).astype(f32)

    def turn(m, carry):
        fs[m] = fsrc[pl.ds(m, FEAT, stride=SRC), :].T.astype(bf16)
        return carry

    lax.fori_loop(0, SRC, turn, 0)

    def weights(leaf, rhs):
        y = nn(fs[leaf], rhs)
        inv = lax.rsqrt(y[:, :PAN])
        k = y[:, PAN:] * (inv * inv * inv)
        hi = k.astype(bf16)
        lo = (k - hi.astype(f32)).astype(bf16)
        return jnp.concatenate([hi, lo], 1)

    def one_leaf(n, carry):
        rhs = jnp.concatenate(
            [ftar[0, pl.ds(n, FEAT, stride=LEAF), :], ftar[1, pl.ds(n, FEAT, stride=LEAF), :]], 1
        ).astype(bf16)
        total = count[n]

        def pair(i, acc):
            second = 2 * i + 1
            live = second < total
            m1 = index[n, 2 * i]
            m2 = jnp.where(live, index[n, jnp.minimum(second, index.shape[1] - 1)], m1)
            scale = jnp.where(live, 1.0, 0.0).astype(f32)
            both = jnp.concatenate([weights(m1, rhs), weights(m2, rhs)], 0)
            d1 = dtab[pl.ds(pl.multiple_of(m1 * 8, 8), 8), :]
            d2 = dtab[pl.ds(pl.multiple_of(m2 * 8, 8), 8), :] * scale
            d = jnp.concatenate([d1, d2], 1).astype(bf16)
            return acc + nn(d, both)

        acc = lax.fori_loop(0, (total + 1) // 2, pair, jnp.zeros((8, 2 * PAN), f32))
        acc = acc[:, :PAN] + acc[:, PAN:]
        out[pl.ds(n, RHS, stride=LEAF), :] = acc[:RHS] + acc[RHS:]
        return carry

    lax.fori_loop(0, LEAF, one_leaf, 0)


def near(index, count, cen, nrm, dens, low, high):
    return pl.pallas_call(
        near_kernel,
        in_specs=[SM, SM] + [VM] * 5,
        out_specs=VM,
        out_shape=jax.ShapeDtypeStruct((ROWS, PAN), f32),
        scratch_shapes=[
            pltpu.VMEM((10, SRC, PAN), f32),
            pltpu.VMEM((FEAT * SRC, PAN), f32),
            pltpu.VMEM((2, FEAT * LEAF, PAN), f32),
            pltpu.VMEM((SRC, PAN, FEAT), bf16),
            pltpu.VMEM((SRC * 8, PAN), f32),
        ],
        compiler_params=pltpu.CompilerParams(vmem_limit_bytes=24 * MIB),
        cost_estimate=pl.CostEstimate(
            flops=20_000_000_00, bytes_accessed=1_000_000, transcendentals=3_600_000
        ),
        name="near",
    )(index, count, cen, nrm, dens, low, high)


def finish_kernel(
    par, octs, slots, kinds, arrived, tables, l2l, tp, near_part, out, turned, picked, s0, s1, s2, acc
):
    step = pl.program_id(0)
    spread = (s0, s1, s2)
    groups = slots.shape[0]

    @pl.when(step == 0)
    def _():
        acc[...] = jnp.zeros_like(acc)
        for t in range(BOX // PAN):
            turned[PAN * t : PAN * (t + 1), :] = arrived[:, PAN * t : PAN * (t + 1)].T
        slot_row = iota((128 * SLOT, PAN), 0)

        def pick(g, carry):
            hot = (slot_row == slots[pl.ds(g, 1), :]).astype(f32).astype(bf16)
            picked[g] = nn(turned[: RHS * EQ, :], hot).astype(bf16)
            return carry

        lax.fori_loop(0, groups, pick, 0)

        def build(g, per, base):
            kind = jnp.broadcast_to(kinds[pl.ds(g, 1), :], (PAN, PAN)).T
            src = picked[g]
            for h in range(per):
                target = kind - h * OPSP
                hot = jnp.concatenate(
                    [
                        (target == iota((PAN, PAN), 1) + PAN * t).astype(f32).astype(bf16)
                        for t in range(3)
                    ],
                    1,
                )
                y = nn(src, hot)
                for r in range(RHS):
                    at = pl.multiple_of((base + r * LEAF + h) * EQ, 8)
                    for t in range(3):
                        spread[t][pl.ds(at, EQ), :] = y[
                            r * EQ : (r + 1) * EQ, PAN * t : PAN * (t + 1)
                        ]

        def far_group(g, carry):
            build(g, 2, g * 2)
            return carry

        def top_group(g, carry):
            build(g, 4, ROWS + (g - 8) * 4)
            return carry

        lax.fori_loop(0, 8, far_group, 0)
        lax.fori_loop(8, 12, top_group, 0)

    left = []
    right = []
    for i in range(FB):
        for t in range(3):
            left.append(spread[t][pl.ds(step * FB + i, 2 * ROWS, stride=EQ), :].astype(bf16))
        right.append(tables[i])
    acc[...] += nt(jnp.concatenate(left, 1), jnp.concatenate(right, 1))

    @pl.when(step == pl.num_programs(0) - 1)
    def _():
        far = acc[:ROWS, :EQ]
        top = acc[ROWS:, :EQ].astype(bf16)
        row = iota((ROWS, ROWS), 0)
        lane = iota((ROWS, ROWS), 1)
        parent = jnp.zeros((ROWS, ROWS), i32)
        for n in range(LEAF):
            parent = jnp.where(row % LEAF == n, par[0, n], parent)
        hit = (parent == lane % LEAF) & (row // LEAF == lane // LEAF)
        chosen = nn(hit.astype(f32).astype(bf16), top).astype(bf16)
        leaf_row = iota((ROWS, EQ), 0) % LEAF
        down = jnp.zeros((ROWS, EQ), f32)
        for n in range(LEAF):
            down = jnp.where(leaf_row == n, nt(chosen, l2l[octs[0, n]]), down)
        local = (down + far).astype(bf16)
        leaf_row = iota((ROWS, PAN), 0) % LEAF
        res = jnp.zeros((ROWS, PAN), f32)
        for n in range(LEAF):
            res = jnp.where(leaf_row == n, nn(local, tp[n]), res)
        out[...] = res + near_part[...]


def finish(par, octs, slots, kinds, arrived, tables, l2l, tp, near_part):
    def whole(x):
        return pl.BlockSpec(x.shape, lambda i: (0,) * x.ndim)

    sm = pl.BlockSpec(memory_space=pltpu.SMEM)
    return pl.pallas_call(
        finish_kernel,
        grid=(EQ // FB,),
        in_specs=[
            sm,
            sm,
            whole(slots),
            whole(kinds),
            whole(arrived),
            pl.BlockSpec((FB, EQP, OPSP), lambda i: (i, 0, 0)),
            whole(l2l),
            whole(tp),
            whole(near_part),
        ],
        out_specs=pl.BlockSpec((ROWS, PAN), lambda i: (0, 0)),
        out_shape=jax.ShapeDtypeStruct((ROWS, PAN), f32),
        scratch_shapes=[
            pltpu.VMEM((BOX, 128 * SLOT), bf16),
            pltpu.VMEM((12, RHS * EQ, PAN), bf16),
            pltpu.VMEM((2 * ROWS * EQ, PAN), f32),
            pltpu.VMEM((2 * ROWS * EQ, PAN), f32),
            pltpu.VMEM((2 * ROWS * EQ, PAN), f32),
            pltpu.VMEM((2 * ROWS, EQP), f32),
        ],
        compiler_params=pltpu.CompilerParams(vmem_limit_bytes=56 * MIB),
        name="finish",
    )(par, octs, slots, kinds, arrived, tables, l2l, tp, near_part)


def per_device(
    density,
    centres,
    normal,
    to_multipole,
    to_panels,
    m2m_ops,
    l2l_ops,
    m2l_ops,
    near_index,
    near_count,
    send_box,
    send_count,
    far_slot,
    far_op,
    far_count,
    parent_of,
    octant,
    top_src,
    top_op,
    top_count,
):
    dens = density.reshape(ROWS, PAN)
    mult, part, low, high = upward(parent_of, octant, dens, centres, normal, to_multipole, m2m_ops)

    axes = ("leaf", "sub")
    count = lax.axis_size("leaf") * lax.axis_size("sub")
    forward = [(i, i + 1) for i in range(count - 1)]
    backward = [(i + 1, i) for i in range(count - 1)]
    low = lax.ppermute(low, axes, forward)
    high = lax.ppermute(high, axes, backward)

    pieces = lax.all_to_all(part, "sub", split_axis=0, concat_axis=0, tiled=True)

    slot_id = jnp.arange(2, dtype=i32)[None, :]
    far_ids = jnp.where(slot_id < send_count[0][:, None], send_box[0], -1)
    own_ids = jnp.broadcast_to(
        jnp.array([16, 17, 18, 19, -1, -1], i32)[None, :], (count, SLOT - 2)
    )
    ids = jnp.concatenate([far_ids, own_ids], 1).reshape(count * SLOT, 1)
    outgoing = pack(ids, mult, pieces)
    arrived = lax.all_to_all(outgoing, axes, split_axis=0, concat_axis=0, tiled=True)

    tables = reorder(jnp.transpose(m2l_ops, (1, 2, 0)))
    near_part = near(near_index, near_count, centres, normal, dens, low, high)

    far_live = jnp.arange(far_slot.shape[1])[None, :] < far_count[:, None]
    far_rows = jnp.where(far_live, (far_slot // 2) * SLOT + far_slot % 2, -1)
    top_live = jnp.arange(top_src.shape[1])[None, :] < top_count[:, None]
    top_rows = jnp.where(top_live, (top_src // 4) * SLOT + 2 + top_src % 4, -1)
    slots = jnp.concatenate([far_rows.reshape(8, PAN), top_rows.reshape(4, PAN)], 0)
    far_kind = far_op + OPSP * (jnp.arange(LEAF, dtype=i32) % 2)[:, None]
    top_kind = top_op + OPSP * (jnp.arange(LEAF, dtype=i32) % 4)[:, None]
    kinds = jnp.concatenate([far_kind.reshape(8, PAN), top_kind.reshape(4, PAN)], 0)

    res = finish(
        parent_of,
        octant,
        slots,
        kinds,
        arrived,
        tables,
        l2l_ops,
        jnp.transpose(to_panels, (0, 2, 1)),
        near_part,
    )
    return res.reshape(RHS, LEAF, PAN)


def solution(mesh):
    both = ("leaf", "sub")
    return jax.shard_map(
        per_device,
        mesh=mesh,
        in_specs=(
            P(None, both, None),
            P(None, both, None),
            P(None, both, None),
            P(both, None, None),
            P(both, None, None),
            P(),
            P(),
            P(),
            P(both, None),
            P(both),
            P(both, None, None),
            P(both, None),
            P(both, None),
            P(both, None),
            P(both),
            P("leaf", "sub"),
            P("leaf", "sub"),
            P("leaf", None),
            P("leaf", None),
            P("leaf"),
        ),
        out_specs=P(None, both, None),
        check_vma=False,
    )
```

```python
import jax
import jax.numpy as jnp
from jax import lax
from jax.experimental import pallas as pl
from jax.experimental.pallas import tpu as pltpu
from jax.sharding import PartitionSpec as P

f32 = jnp.float32
bf16 = jnp.bfloat16
i32 = jnp.int32

RIM = 4
LEAF = 16
RHS = 4
ROWS = RHS * LEAF
EQ = 152
OPSP = 384
PAN = 128
BOX = 640
SLOT = 8
EPS = 0.01
FB = 16
MIB = 1 << 20
BIG = 56 * MIB

SM = pl.BlockSpec(memory_space=pltpu.SMEM)


def nt(a, b, **kw):
    return lax.dot_general(a, b, (((1,), (1,)), ((), ())), preferred_element_type=f32, **kw)


def nn(a, b, **kw):
    return lax.dot_general(a, b, (((1,), (0,)), ((), ())), preferred_element_type=f32, **kw)


def whole(x):
    return pl.BlockSpec(x.shape, lambda i: (0,) * len(x.shape))


def iota(shape, dim):
    return lax.broadcasted_iota(i32, shape, dim)


def upward_kernel(par, octs, dens, cen, nrm, tm, m2m, mult_out, part_out, low_out, high_out):
    d = dens[...].astype(bf16)
    leaf_row = iota((ROWS, EQ), 0) % LEAF
    mult = jnp.zeros((ROWS, EQ), f32)
    for n in range(LEAF):
        mult = jnp.where(leaf_row == n, nt(d, tm[n]), mult)
    mb = mult.astype(bf16)
    mult_out[...] = mb
    child = jnp.zeros((ROWS, EQ), f32)
    for n in range(LEAF):
        child = jnp.where(leaf_row == n, nt(mb, m2m[octs[0, n]]), child)
    row = iota((ROWS, ROWS), 0)
    lane = iota((ROWS, ROWS), 1)
    parent = jnp.zeros((ROWS, ROWS), i32)
    for n in range(LEAF):
        parent = jnp.where(lane % LEAF == n, par[0, n], parent)
    box = (row // 16) * 4 + row % 4
    hit = (parent == box) & ((row // 4) % 4 == lane // LEAF)
    part_out[...] = nn(hit.astype(f32), child, precision=lax.Precision.HIGHEST)
    for a in range(3):
        high_out[4 * a : 4 * a + 4, :] = cen[a, :RIM, :]
        low_out[4 * a : 4 * a + 4, :] = cen[a, LEAF - RIM :, :]
        high_out[12 + 4 * a : 16 + 4 * a, :] = nrm[a, :RIM, :]
        low_out[12 + 4 * a : 16 + 4 * a, :] = nrm[a, LEAF - RIM :, :]
    for r in range(RHS):
        high_out[24 + 4 * r : 28 + 4 * r, :] = dens[LEAF * r : LEAF * r + RIM, :]
        low_out[24 + 4 * r : 28 + 4 * r, :] = dens[LEAF * (r + 1) - RIM : LEAF * (r + 1), :]


def upward(par, octs, dens, cen, nrm, tm, m2m):
    outs = [
        jax.ShapeDtypeStruct((ROWS, EQ), bf16),
        jax.ShapeDtypeStruct((ROWS, EQ), f32),
        jax.ShapeDtypeStruct((40, PAN), f32),
        jax.ShapeDtypeStruct((40, PAN), f32),
    ]
    return pl.pallas_call(
        upward_kernel,
        grid=(1,),
        in_specs=[SM, SM] + [whole(x) for x in (dens, cen, nrm, tm, m2m)],
        out_specs=[whole(x) for x in outs],
        out_shape=outs,
        compiler_params=pltpu.CompilerParams(vmem_limit_bytes=BIG),
        name="upward",
    )(par, octs, dens, cen, nrm, tm, m2m)


def pack_kernel(ids, mult, pieces, out):
    row = iota((EQ, BOX), 0)
    lane = iota((EQ, BOX), 1)
    own = pieces[0:16, :]
    for s in range(1, 4):
        own = own + pieces[16 * s : 16 * s + 16, :]
    own = own.astype(bf16).astype(f32)
    mf = mult[...].astype(f32)
    table = jnp.zeros((24, BOX), f32)
    for r in range(RHS):
        both = jnp.concatenate(
            [mf[16 * r : 16 * r + 16], own[4 * r : 4 * r + 4], jnp.zeros((4, EQ), f32)], 0
        )
        place = (lane == row + EQ * r).astype(f32).astype(bf16)
        table = table + nn(both.astype(bf16), place)
    hot = (ids[...] == iota((128 * SLOT, 24), 1)).astype(f32).astype(bf16)
    out[...] = nn(hot, table.astype(bf16)).astype(bf16)


def pack(ids, mult, pieces):
    outs = jax.ShapeDtypeStruct((128 * SLOT, BOX), bf16)
    return pl.pallas_call(
        pack_kernel,
        grid=(1,),
        in_specs=[whole(x) for x in (ids, mult, pieces)],
        out_specs=whole(outs),
        out_shape=outs,
        compiler_params=pltpu.CompilerParams(vmem_limit_bytes=BIG),
        name="pack",
    )(ids, mult, pieces)


SRC = LEAF + 2 * RIM
BATCH = 4
FEAT = 48
ORDERS = ((0, 0), (0, 1), (1, 0), (0, 2), (1, 1), (2, 0))


def three(x):
    a = x.astype(bf16).astype(f32)
    b = (x - a).astype(bf16).astype(f32)
    c = (x - a - b).astype(bf16).astype(f32)
    return a, b, c


def near_kernel(index, count, cen, nrm, dens, low, high, out, raw, fsrc, ftar, fs, dpar, dwide, ft, sums, dist):
    for q in range(10):
        raw[q, 0:RIM, :] = low[4 * q : 4 * q + 4, :]
        raw[q, RIM + LEAF : SRC, :] = high[4 * q : 4 * q + 4, :]
        if q < 3:
            body = cen[q]
        elif q < 6:
            body = nrm[q - 3]
        else:
            body = dens[LEAF * (q - 6) : LEAF * (q - 5), :]
        raw[q, RIM : RIM + LEAF, :] = body
    xs = [raw[a] - 0.5 for a in range(3)]
    ns = [raw[3 + a] for a in range(3)]
    xt = [cen[a] - 0.5 for a in range(3)]
    xs3 = [three(v) for v in xs]
    ns3 = [three(v) for v in ns]
    xt3 = [three(v) for v in xt]
    ss = three(xs[0] * xs[0] + xs[1] * xs[1] + xs[2] * xs[2] + EPS)
    sn = three(xs[0] * ns[0] + xs[1] * ns[1] + xs[2] * ns[2])
    tt = three(xt[0] * xt[0] + xt[1] * xt[1] + xt[2] * xt[2])
    one_s = jnp.ones((SRC, PAN), f32)
    zero_s = jnp.zeros((SRC, PAN), f32)
    one = jnp.ones((LEAF, PAN), f32)
    zero = jnp.zeros((LEAF, PAN), f32)
    feats = []
    for a in range(3):
        for i, j in ORDERS:
            feats.append((xs3[a][i], -2.0 * xt3[a][j], zero))
            feats.append((ns3[a][i], zero, xt3[a][j]))
    for i in range(3):
        feats.append((ss[i], one, zero))
        feats.append((sn[i], zero, -one))
        feats.append((one_s, tt[i], zero))
    while len(feats) < FEAT:
        feats.append((zero_s, zero, zero))
    for k, (s, t1, t2) in enumerate(feats):
        fsrc[k * SRC : (k + 1) * SRC, :] = s
        ftar[0, k * LEAF : (k + 1) * LEAF, :] = t1
        ftar[1, k * LEAF : (k + 1) * LEAF, :] = t2
    for m in range(SRC):
        fs[m] = fsrc[pl.ds(m, FEAT, stride=SRC), :].T.astype(bf16)
    dcols = iota((16, RHS * PAN), 1) // PAN
    pick_r = (iota((16, RHS * PAN), 0) // 3 == dcols).astype(f32).astype(bf16)
    for r in range(RHS):
        for j, part in enumerate(three(raw[6 + r])):
            dpar[pl.ds(3 * r + j, SRC, stride=16), :] = part
            dpar[pl.ds(12 + j, SRC, stride=16), :] = zero_s
    dpar[pl.ds(15, SRC, stride=16), :] = zero_s
    for m in range(SRC):
        wide = nn(dpar[16 * m : 16 * m + 16, :].T.astype(bf16), pick_r)
        for r in range(RHS):
            dwide[m, r] = wide[:, PAN * r : PAN * (r + 1)]
    dwide[SRC] = jnp.zeros((RHS, PAN, PAN), f32)
    for n in range(LEAF):
        ft[n] = jnp.concatenate(
            [ftar[0, pl.ds(n, FEAT, stride=LEAF), :], ftar[1, pl.ds(n, FEAT, stride=LEAF), :]], 1
        ).astype(bf16)
    sums[...] = jnp.zeros_like(sums)
    dist[:, :, :PAN] = jnp.ones((BATCH, 2 * PAN, PAN), f32)
    dist[:, :, PAN:] = jnp.zeros((BATCH, 2 * PAN, PAN), f32)
    pairs = 0
    for n in range(LEAF):
        pairs = pairs + (count[n] + 1) // 2
    steps = (pairs + BATCH - 1) // BATCH + 1

    def step(_, carry):
        n, i = carry[0], carry[1]
        old = carry[2:]
        for u in range(BATCH):
            n1, p1, q1 = old[3 * u], old[3 * u + 1], old[3 * u + 2]
            inv = lax.rsqrt(dist[u, :, :PAN])
            k = dist[u, :, PAN:] * (inv * inv * inv)
            for r in range(RHS):
                term = k[:PAN] * dwide[p1, r] + k[PAN:] * dwide[q1, r]
                sums[n1, r] += jnp.sum(term.reshape(PAN // 8, 8, PAN), 0)
        fresh = []
        for u in range(BATCH):
            at = jnp.minimum(n, LEAF - 1)
            first = 2 * i
            live1 = n < LEAF
            live2 = live1 & (first + 1 < count[at])
            p = index[at, first]
            q = index[at, jnp.minimum(first + 1, index.shape[1] - 1)]
            dist[u] = nn(jnp.concatenate([fs[p], fs[q]], 0), ft[at])
            fresh += [at, jnp.where(live1, p, SRC), jnp.where(live2, q, SRC)]
            more = live1 & (first + 2 < count[at])
            n = jnp.where(more, n, n + 1)
            i = jnp.where(more, i + 1, 0)
        return (n, i) + tuple(fresh)

    start = [jnp.int32(0), jnp.int32(0)] + [jnp.int32(0), jnp.int32(SRC), jnp.int32(SRC)] * BATCH
    lax.fori_loop(0, steps, step, tuple(start))
    for r in range(RHS):
        out[LEAF * r : LEAF * (r + 1), :] = jnp.sum(sums[:, r], 1)


def near(index, count, cen, nrm, dens, low, high):
    outs = jax.ShapeDtypeStruct((ROWS, PAN), f32)
    return pl.pallas_call(
        near_kernel,
        grid=(1,),
        in_specs=[SM, SM] + [whole(x) for x in (cen, nrm, dens, low, high)],
        out_specs=whole(outs),
        out_shape=outs,
        scratch_shapes=[
            pltpu.VMEM((10, SRC, PAN), f32),
            pltpu.VMEM((FEAT * SRC, PAN), f32),
            pltpu.VMEM((2, FEAT * LEAF, PAN), f32),
            pltpu.VMEM((SRC, PAN, FEAT), bf16),
            pltpu.VMEM((SRC * 16, PAN), f32),
            pltpu.VMEM((SRC + 1, RHS, PAN, PAN), f32),
            pltpu.VMEM((LEAF, FEAT, 2 * PAN), bf16),
            pltpu.VMEM((LEAF, RHS, 8, PAN), f32),
            pltpu.VMEM((BATCH, 2 * PAN, 2 * PAN), f32),
        ],
        compiler_params=pltpu.CompilerParams(vmem_limit_bytes=BIG),
        cost_estimate=pl.CostEstimate(
            flops=20_000_000_00, bytes_accessed=1_000_000, transcendentals=3_600_000
        ),
        name="near",
    )(index, count, cen, nrm, dens, low, high)


def finish_kernel(
    par, octs, slots, kinds, arrived, ops0, ops1, l2l, tp, near_part, out,
    turned, picked, s0, s1, s2, m0, m1, m2, m3, m4, m5, acc,
):
    step = pl.program_id(0)
    spread = (s0, s1, s2)
    even = (m0, m1, m2)
    odd = (m3, m4, m5)
    tail = ops0.shape[2] - 2 * PAN

    @pl.when(step == 0)
    def _():
        acc[...] = jnp.zeros_like(acc)
        m2[...] = jnp.zeros_like(m2)
        m5[...] = jnp.zeros_like(m5)
        for t in range(BOX // PAN):
            turned[PAN * t : PAN * (t + 1), :] = arrived[:, PAN * t : PAN * (t + 1)].T
        slot_row = iota((128 * SLOT, 2 * PAN), 0)

        def pick(g, carry):
            hot = (slot_row == slots[pl.ds(g, 1), :]).astype(f32).astype(bf16)
            picked[g] = nn(turned[: RHS * EQ, :], hot).astype(bf16)
            return carry

        lax.fori_loop(0, slots.shape[0], pick, 0)

        def build(g, half, per, base):
            ids = kinds[pl.ds(g, 1), :][:, PAN * half : PAN * (half + 1)]
            kind = jnp.broadcast_to(ids, (PAN, PAN)).T
            src = picked[g, :, PAN * half : PAN * (half + 1)]
            for h in range(0, per, 2):
                hot = jnp.concatenate(
                    [
                        (kind == iota((PAN, PAN), 1) + (PAN * t + h * OPSP)).astype(f32).astype(bf16)
                        for t in range(6)
                    ],
                    1,
                )
                y = nn(src, hot)
                for r in range(RHS):
                    for u in range(2):
                        at = pl.multiple_of((base + r * LEAF + h + u) * EQ, 8)
                        for t in range(3):
                            spread[t][pl.ds(at, EQ), :] = y[
                                r * EQ : (r + 1) * EQ, PAN * (t + 3 * u) : PAN * (t + 3 * u + 1)
                            ]

        def far_group(g, carry):
            build(g, 0, 2, g * 4)
            build(g, 1, 2, g * 4 + 2)
            return carry

        def top_group(g, carry):
            build(g, 0, 4, ROWS + (g - 4) * 8)
            build(g, 1, 4, ROWS + (g - 4) * 8 + 4)
            return carry

        lax.fori_loop(0, 4, far_group, 0)
        lax.fori_loop(4, 6, top_group, 0)

    def move(to):
        for h, ops in enumerate((ops0, ops1)):
            rows = ops.shape[0] * 8
            for g in range(FB // 8):
                at = slice(g * 8 * EQ + h * rows, g * 8 * EQ + (h + 1) * rows)
                part = ops[:, 8 * g : 8 * g + 8, :].astype(f32).reshape(rows, ops.shape[2])
                for t in range(2):
                    to[t][at, :] = part[:, PAN * t : PAN * (t + 1)]
                to[2][at, :tail] = part[:, 2 * PAN :]

    def multiply(width, of):
        base = (step - 1) * FB
        left = []
        right = []
        for i in range(width):
            for t in range(3):
                left.append(spread[t][pl.ds(base + i, 2 * ROWS, stride=EQ), :].astype(bf16))
                right.append(of[t][pl.ds(i // 8 * 8 * EQ + i % 8, EQ, stride=8), :].astype(bf16))
        acc[...] += nt(jnp.concatenate(right, 1), jnp.concatenate(left, 1))

    last = pl.num_programs(0) - 1

    @pl.when(step == 0)
    def _():
        move(even)

    @pl.when((step > 0) & (step < last) & (step % 2 == 1))
    def _():
        multiply(FB, even)
        move(odd)

    @pl.when((step > 0) & (step < last) & (step % 2 == 0))
    def _():
        multiply(FB, odd)
        move(even)

    @pl.when(step == last)
    def _():
        multiply(EQ % FB, odd)
        res = acc[...].T
        far = res[:ROWS]
        top = res[ROWS:].astype(bf16)
        row = iota((ROWS, ROWS), 0)
        lane = iota((ROWS, ROWS), 1)
        parent = jnp.zeros((ROWS, ROWS), i32)
        for n in range(LEAF):
            parent = jnp.where(row % LEAF == n, par[0, n], parent)
        hit = (parent == lane % LEAF) & (row // LEAF == lane // LEAF)
        chosen = nn(hit.astype(f32).astype(bf16), top).astype(bf16)
        leaf_row = iota((ROWS, EQ), 0) % LEAF
        down = jnp.zeros((ROWS, EQ), f32)
        for n in range(LEAF):
            down = jnp.where(leaf_row == n, nt(chosen, l2l[octs[0, n]]), down)
        local = (down + far).astype(bf16)
        leaf_row = iota((ROWS, PAN), 0) % LEAF
        res = jnp.zeros((ROWS, PAN), f32)
        for n in range(LEAF):
            res = jnp.where(leaf_row == n, nn(local, tp[n]), res)
        out[...] = res + near_part[...]


def finish(par, octs, slots, kinds, arrived, tables, l2l, tp, near_part):
    chunks = pl.cdiv(EQ, FB)
    half = (EQ // 2, FB, tables.shape[2])
    return pl.pallas_call(
        finish_kernel,
        grid=(chunks + 1,),
        in_specs=[
            SM,
            SM,
            whole(slots),
            whole(kinds),
            whole(arrived),
            pl.BlockSpec(half, lambda i: (0, jnp.minimum(i, chunks - 1), 0)),
            pl.BlockSpec(half, lambda i: (1, jnp.minimum(i, chunks - 1), 0)),
            whole(l2l),
            whole(tp),
            whole(near_part),
        ],
        out_specs=pl.BlockSpec((ROWS, PAN), lambda i: (0, 0)),
        out_shape=jax.ShapeDtypeStruct((ROWS, PAN), f32),
        scratch_shapes=[
            pltpu.VMEM((BOX, 128 * SLOT), bf16),
            pltpu.VMEM((6, RHS * EQ, 2 * PAN), bf16),
            pltpu.VMEM((2 * ROWS * EQ, PAN), f32),
            pltpu.VMEM((2 * ROWS * EQ, PAN), f32),
            pltpu.VMEM((2 * ROWS * EQ, PAN), f32),
            pltpu.VMEM((EQ * FB, PAN), f32),
            pltpu.VMEM((EQ * FB, PAN), f32),
            pltpu.VMEM((EQ * FB, PAN), f32),
            pltpu.VMEM((EQ * FB, PAN), f32),
            pltpu.VMEM((EQ * FB, PAN), f32),
            pltpu.VMEM((EQ * FB, PAN), f32),
            pltpu.VMEM((EQ, 2 * ROWS), f32),
        ],
        compiler_params=pltpu.CompilerParams(vmem_limit_bytes=BIG),
        name="finish",
    )(par, octs, slots, kinds, arrived, tables, tables, l2l, tp, near_part)


def per_device(
    density,
    centres,
    normal,
    to_multipole,
    to_panels,
    m2m_ops,
    l2l_ops,
    m2l_ops,
    near_index,
    near_count,
    send_box,
    send_count,
    far_slot,
    far_op,
    far_count,
    parent_of,
    octant,
    top_src,
    top_op,
    top_count,
):
    dens = density.reshape(ROWS, PAN)
    mult, part, low, high = upward(parent_of, octant, dens, centres, normal, to_multipole, m2m_ops)

    axes = ("leaf", "sub")
    count = lax.axis_size("leaf") * lax.axis_size("sub")
    forward = [(i, i + 1) for i in range(count - 1)]
    backward = [(i + 1, i) for i in range(count - 1)]
    low = lax.ppermute(low, axes, forward)
    high = lax.ppermute(high, axes, backward)

    pieces = lax.all_to_all(part, "sub", split_axis=0, concat_axis=0, tiled=True)

    slot_id = jnp.arange(2, dtype=i32)[None, :]
    far_ids = jnp.where(slot_id < send_count[0][:, None], send_box[0], -1)
    own_ids = jnp.broadcast_to(
        jnp.array([16, 17, 18, 19, -1, -1], i32)[None, :], (count, SLOT - 2)
    )
    ids = jnp.concatenate([far_ids, own_ids], 1).reshape(count * SLOT, 1)
    outgoing = pack(ids, mult, pieces)
    arrived = lax.all_to_all(outgoing, axes, split_axis=0, concat_axis=0, tiled=True)

    near_part = near(near_index, near_count, centres, normal, dens, low, high)

    far_live = jnp.arange(far_slot.shape[1])[None, :] < far_count[:, None]
    far_rows = jnp.where(far_live, (far_slot // 2) * SLOT + far_slot % 2, -1)
    top_live = jnp.arange(top_src.shape[1])[None, :] < top_count[:, None]
    top_rows = jnp.where(top_live, (top_src // 4) * SLOT + 2 + top_src % 4, -1)
    slots = jnp.concatenate([far_rows.reshape(4, 2 * PAN), top_rows.reshape(2, 2 * PAN)], 0)
    far_kind = far_op + OPSP * (jnp.arange(LEAF, dtype=i32) % 2)[:, None]
    top_kind = top_op + OPSP * (jnp.arange(LEAF, dtype=i32) % 4)[:, None]
    kinds = jnp.concatenate([far_kind.reshape(4, 2 * PAN), top_kind.reshape(2, 2 * PAN)], 0)

    res = finish(
        parent_of,
        octant,
        slots,
        kinds,
        arrived,
        jnp.transpose(m2l_ops, (1, 2, 0)),
        l2l_ops,
        jnp.transpose(to_panels, (0, 2, 1)),
        near_part,
    )
    return res.reshape(RHS, LEAF, PAN)


def solution(mesh):
    both = ("leaf", "sub")
    return jax.shard_map(
        per_device,
        mesh=mesh,
        in_specs=(
            P(None, both, None),
            P(None, both, None),
            P(None, both, None),
            P(both, None, None),
            P(both, None, None),
            P(),
            P(),
            P(),
            P(both, None),
            P(both),
            P(both, None, None),
            P(both, None),
            P(both, None),
            P(both, None),
            P(both),
            P("leaf", "sub"),
            P("leaf", "sub"),
            P("leaf", None),
            P("leaf", None),
            P("leaf"),
        ),
        out_specs=P(None, both, None),
        check_vma=False,
    )
```

```python
import jax
import jax.numpy as jnp
from jax import lax
from jax.experimental import pallas as pl
from jax.experimental.pallas import tpu as pltpu
from jax.sharding import PartitionSpec as P

f32 = jnp.float32
bf16 = jnp.bfloat16
i32 = jnp.int32

RIM = 4
LEAF = 16
RHS = 4
ROWS = RHS * LEAF
EQ = 152
OPSP = 384
PAN = 128
BOX = 640
PIECES = 5
CHUNK = 32
PITCH = 40
EPS = 0.01
FB = 16
MIB = 1 << 20
BIG = 56 * MIB

SM = pl.BlockSpec(memory_space=pltpu.SMEM)


def nt(a, b, **kw):
    return lax.dot_general(a, b, (((1,), (1,)), ((), ())), preferred_element_type=f32, **kw)


def nn(a, b, **kw):
    return lax.dot_general(a, b, (((1,), (0,)), ((), ())), preferred_element_type=f32, **kw)


def whole(x):
    return pl.BlockSpec(x.shape, lambda i: (0,) * len(x.shape))


def iota(shape, dim):
    return lax.broadcasted_iota(i32, shape, dim)


def upward_kernel(par, octs, dens, cen, nrm, tm, m2m, mult_out, c0, c1, c2, c3, low_out, high_out):
    d = dens[...].astype(bf16)
    leaf_row = iota((ROWS, EQ), 0) % LEAF
    mult = jnp.zeros((ROWS, EQ), f32)
    for n in range(LEAF):
        mult = jnp.where(leaf_row == n, nt(d, tm[n]), mult)
    mb = mult.astype(bf16)
    mult_out[...] = mb
    child = jnp.zeros((ROWS, EQ), f32)
    for n in range(LEAF):
        child = jnp.where(leaf_row == n, nt(mb, m2m[octs[0, n]]), child)
    row = iota((ROWS, ROWS), 0)
    lane = iota((ROWS, ROWS), 1)
    parent = jnp.zeros((ROWS, ROWS), i32)
    for n in range(LEAF):
        parent = jnp.where(lane % LEAF == n, par[0, n], parent)
    box = ((row // 16 + lax.axis_index("sub")) % 4) * 4 + row % 4
    hit = (parent == box) & ((row // 4) % 4 == lane // LEAF)
    part = nn(hit.astype(f32), child, precision=lax.Precision.HIGHEST)
    for s, piece in enumerate((c0, c1, c2, c3)):
        piece[...] = part[16 * s : 16 * s + 16]
    for a in range(3):
        high_out[4 * a : 4 * a + 4, :] = cen[a, :RIM, :]
        low_out[4 * a : 4 * a + 4, :] = cen[a, LEAF - RIM :, :]
        high_out[12 + 4 * a : 16 + 4 * a, :] = nrm[a, :RIM, :]
        low_out[12 + 4 * a : 16 + 4 * a, :] = nrm[a, LEAF - RIM :, :]
    for r in range(RHS):
        high_out[24 + 4 * r : 28 + 4 * r, :] = dens[LEAF * r : LEAF * r + RIM, :]
        low_out[24 + 4 * r : 28 + 4 * r, :] = dens[LEAF * (r + 1) - RIM : LEAF * (r + 1), :]
def upward(par, octs, dens, cen, nrm, tm, m2m):
    outs = [
        jax.ShapeDtypeStruct((ROWS, EQ), bf16),
    ]
    outs += [jax.ShapeDtypeStruct((16, EQ), f32)] * 4
    outs += [jax.ShapeDtypeStruct((40, PAN), f32)] * 2
    return pl.pallas_call(
        upward_kernel,
        grid=(1,),
        in_specs=[SM, SM] + [whole(x) for x in (dens, cen, nrm, tm, m2m)],
        out_specs=[whole(x) for x in outs],
        out_shape=outs,
        compiler_params=pltpu.CompilerParams(vmem_limit_bytes=BIG),
        name="upward",
    )(par, octs, dens, cen, nrm, tm, m2m)


def pack_kernel(boxes, counts, mult, c0, c1, c2, c3, low, high, out, far, const):
    row = iota((EQ, BOX), 0)
    lane = iota((EQ, BOX), 1)
    own = (c0[...] + c1[...]) + (c2[...] + c3[...])
    own = own.astype(bf16).astype(f32)
    mf = mult[...].astype(f32)
    table = jnp.zeros((24, BOX), f32)
    for r in range(RHS):
        both = jnp.concatenate(
            [mf[16 * r : 16 * r + 16], own[4 * r : 4 * r + 4], jnp.zeros((4, EQ), f32)], 0
        )
        place = (lane == row + EQ * r).astype(f32).astype(bf16)
        table = table + nn(both.astype(bf16), place)
    leaf = iota((LEAF, PAN), 0)
    for j in range(2):
        hot = ((boxes[j : j + 1, :] == leaf) & (counts[...] > j)).astype(f32).T
        y = nn(hot.astype(bf16), table[:LEAF].astype(bf16))
        for t in range(PIECES):
            far[pl.ds(PIECES * j + t, PAN, stride=24), :] = y[:, PAN * t : PAN * (t + 1)]
    const[...] = jnp.zeros_like(const)
    for q in range(4):
        for t in range(PIECES):
            at = PIECES * (2 + q) + t
            const[at : at + 1, :] = table[LEAF + q : LEAF + q + 1, PAN * t : PAN * (t + 1)]
    head = const[:16]
    rest = const[16:].astype(bf16)
    is_far = iota((16, PAN), 0) < 2 * PIECES
    for d in range(PAN):
        out[CHUNK * d : CHUNK * d + 16, :] = jnp.where(
            is_far, far[24 * d : 24 * d + 16, :], head
        ).astype(bf16)
        out[CHUNK * d + 16 : CHUNK * (d + 1), :] = rest


def pack(boxes, counts, mult, pieces, later):
    outs = jax.ShapeDtypeStruct((PAN * CHUNK, PAN), bf16)
    return pl.pallas_call(
        pack_kernel,
        grid=(1,),
        in_specs=[whole(x) for x in (boxes, counts, mult, *pieces)]
        + [pl.BlockSpec(memory_space=pl.ANY)] * len(later),
        out_specs=whole(outs),
        out_shape=outs,
        scratch_shapes=[pltpu.VMEM((PAN * 24, PAN), f32), pltpu.VMEM((CHUNK, PAN), f32)],
        compiler_params=pltpu.CompilerParams(vmem_limit_bytes=BIG),
        name="pack",
    )(boxes, counts, mult, *pieces, *later)


SRC = LEAF + 2 * RIM
BATCH = 4
FEAT = 48
ORDERS = ((0, 0), (0, 1), (1, 0), (0, 2), (1, 1), (2, 0))


def three(x):
    a = x.astype(bf16).astype(f32)
    b = (x - a).astype(bf16).astype(f32)
    c = (x - a - b).astype(bf16).astype(f32)
    return a, b, c


def near_kernel(index, count, cen, nrm, dens, low, high, out, raw, fsrc, ftar, fs, dpar, dwide, ft, sums, dist):
    for q in range(10):
        raw[q, 0:RIM, :] = low[4 * q : 4 * q + 4, :]
        raw[q, RIM + LEAF : SRC, :] = high[4 * q : 4 * q + 4, :]
        if q < 3:
            body = cen[q]
        elif q < 6:
            body = nrm[q - 3]
        else:
            body = dens[LEAF * (q - 6) : LEAF * (q - 5), :]
        raw[q, RIM : RIM + LEAF, :] = body
    xs = [raw[a] - 0.5 for a in range(3)]
    ns = [raw[3 + a] for a in range(3)]
    xt = [cen[a] - 0.5 for a in range(3)]
    xs3 = [three(v) for v in xs]
    ns3 = [three(v) for v in ns]
    xt3 = [three(v) for v in xt]
    ss = three(xs[0] * xs[0] + xs[1] * xs[1] + xs[2] * xs[2] + EPS)
    sn = three(xs[0] * ns[0] + xs[1] * ns[1] + xs[2] * ns[2])
    tt = three(xt[0] * xt[0] + xt[1] * xt[1] + xt[2] * xt[2])
    one_s = jnp.ones((SRC, PAN), f32)
    zero_s = jnp.zeros((SRC, PAN), f32)
    one = jnp.ones((LEAF, PAN), f32)
    zero = jnp.zeros((LEAF, PAN), f32)
    feats = []
    for a in range(3):
        for i, j in ORDERS:
            feats.append((xs3[a][i], -2.0 * xt3[a][j], zero))
            feats.append((ns3[a][i], zero, xt3[a][j]))
    for i in range(3):
        feats.append((ss[i], one, zero))
        feats.append((sn[i], zero, -one))
        feats.append((one_s, tt[i], zero))
    while len(feats) < FEAT:
        feats.append((zero_s, zero, zero))
    for k, (s, t1, t2) in enumerate(feats):
        fsrc[k * SRC : (k + 1) * SRC, :] = s
        ftar[0, k * LEAF : (k + 1) * LEAF, :] = t1
        ftar[1, k * LEAF : (k + 1) * LEAF, :] = t2
    for m in range(SRC):
        fs[m] = fsrc[pl.ds(m, FEAT, stride=SRC), :].T.astype(bf16)
    dcols = iota((16, RHS * PAN), 1) // PAN
    pick_r = (iota((16, RHS * PAN), 0) // 3 == dcols).astype(f32).astype(bf16)
    for r in range(RHS):
        for j, part in enumerate(three(raw[6 + r])):
            dpar[pl.ds(3 * r + j, SRC, stride=16), :] = part
            dpar[pl.ds(12 + j, SRC, stride=16), :] = zero_s
    dpar[pl.ds(15, SRC, stride=16), :] = zero_s
    for m in range(SRC):
        wide = nn(dpar[16 * m : 16 * m + 16, :].T.astype(bf16), pick_r)
        for r in range(RHS):
            dwide[m, r] = wide[:, PAN * r : PAN * (r + 1)]
    dwide[SRC] = jnp.zeros((RHS, PAN, PAN), f32)
    for n in range(LEAF):
        ft[n] = jnp.concatenate(
            [ftar[0, pl.ds(n, FEAT, stride=LEAF), :], ftar[1, pl.ds(n, FEAT, stride=LEAF), :]], 1
        ).astype(bf16)
    sums[...] = jnp.zeros_like(sums)
    dist[:, :, :PAN] = jnp.ones((BATCH, 2 * PAN, PAN), f32)
    dist[:, :, PAN:] = jnp.zeros((BATCH, 2 * PAN, PAN), f32)
    pairs = 0
    for n in range(LEAF):
        pairs = pairs + (count[n] + 1) // 2
    steps = (pairs + BATCH - 1) // BATCH + 1

    def step(_, carry):
        n, i = carry[0], carry[1]
        old = carry[2:]
        for u in range(BATCH):
            n1, p1, q1 = old[3 * u], old[3 * u + 1], old[3 * u + 2]
            inv = lax.rsqrt(dist[u, :, :PAN])
            k = dist[u, :, PAN:] * (inv * inv * inv)
            for r in range(RHS):
                term = k[:PAN] * dwide[p1, r] + k[PAN:] * dwide[q1, r]
                sums[n1, r] += jnp.sum(term.reshape(PAN // 8, 8, PAN), 0)
        fresh = []
        for u in range(BATCH):
            at = jnp.minimum(n, LEAF - 1)
            first = 2 * i
            live1 = n < LEAF
            live2 = live1 & (first + 1 < count[at])
            p = index[at, first]
            q = index[at, jnp.minimum(first + 1, index.shape[1] - 1)]
            dist[u] = nn(jnp.concatenate([fs[p], fs[q]], 0), ft[at])
            fresh += [at, jnp.where(live1, p, SRC), jnp.where(live2, q, SRC)]
            more = live1 & (first + 2 < count[at])
            n = jnp.where(more, n, n + 1)
            i = jnp.where(more, i + 1, 0)
        return (n, i) + tuple(fresh)

    start = [jnp.int32(0), jnp.int32(0)] + [jnp.int32(0), jnp.int32(SRC), jnp.int32(SRC)] * BATCH
    lax.fori_loop(0, steps, step, tuple(start))
    for r in range(RHS):
        out[LEAF * r : LEAF * (r + 1), :] = jnp.sum(sums[:, r], 1)


def near(index, count, cen, nrm, dens, low, high):
    outs = jax.ShapeDtypeStruct((ROWS, PAN), f32)
    return pl.pallas_call(
        near_kernel,
        grid=(1,),
        in_specs=[SM, SM] + [whole(x) for x in (cen, nrm, dens, low, high)],
        out_specs=whole(outs),
        out_shape=outs,
        scratch_shapes=[
            pltpu.VMEM((10, SRC, PAN), f32),
            pltpu.VMEM((FEAT * SRC, PAN), f32),
            pltpu.VMEM((2, FEAT * LEAF, PAN), f32),
            pltpu.VMEM((SRC, PAN, FEAT), bf16),
            pltpu.VMEM((SRC * 16, PAN), f32),
            pltpu.VMEM((SRC + 1, RHS, PAN, PAN), f32),
            pltpu.VMEM((LEAF, FEAT, 2 * PAN), bf16),
            pltpu.VMEM((LEAF, RHS, 8, PAN), f32),
            pltpu.VMEM((BATCH, 2 * PAN, 2 * PAN), f32),
        ],
        compiler_params=pltpu.CompilerParams(vmem_limit_bytes=BIG),
        cost_estimate=pl.CostEstimate(
            flops=20_000_000_00, bytes_accessed=1_000_000, transcendentals=3_600_000
        ),
        name="near",
    )(index, count, cen, nrm, dens, low, high)


def finish_kernel(
    par, octs, far_count, top_count, far_slot, far_op, top_src, top_op, arrived, ops0, ops1, l2l, tp, near_part, out,
    ids, slots, kinds, turned, picked, s0, s1, s2, m0, m1, m2, m3, m4, m5, acc,
):
    step = pl.program_id(0)
    spread = (s0, s1, s2)
    even = (m0, m1, m2)
    odd = (m3, m4, m5)
    tail = ops0.shape[2] - 2 * PAN

    @pl.when(step == 0)
    def _():
        acc[...] = jnp.zeros_like(acc)
        m2[...] = jnp.zeros_like(m2)
        m5[...] = jnp.zeros_like(m5)
        for p in range(PAN):
            s0[PITCH * p : PITCH * p + CHUNK, :] = arrived[CHUNK * p : CHUNK * (p + 1), :].astype(f32)
        for j in range(6):
            for t in range(PIECES):
                piece = s0[pl.ds(PIECES * j + t, PAN, stride=PITCH), :].T
                turned[PAN * t : PAN * (t + 1), PAN * j : PAN * (j + 1)] = piece.astype(bf16)

        row = iota((LEAF, far_slot.shape[1]), 0)
        lane = iota((LEAF, far_slot.shape[1]), 1)
        live = jnp.zeros(row.shape, i32)
        for n in range(LEAF):
            live = jnp.where(row == n, far_count[n], live)
        slot = far_slot[...]
        ids[...] = jnp.where(lane < live, (slot % 2) * PAN + slot // 2, -1)
        slots[0:4, :] = jnp.concatenate([ids[pl.ds(h, 4, stride=4), :] for h in range(4)], 1)
        kinds[0:4, :] = jnp.concatenate(
            [far_op[pl.ds(h, 4, stride=4), :] + OPSP * (h % 2) for h in range(4)], 1
        )
        row = iota((LEAF, top_src.shape[1]), 0)
        lane = iota((LEAF, top_src.shape[1]), 1)
        live = jnp.zeros(row.shape, i32)
        for n in range(LEAF):
            live = jnp.where(row == n, top_count[n], live)
        slot = top_src[...]
        ids[:, : row.shape[1]] = jnp.where(lane < live, (slot % 4) * PAN + slot // 4, -1)
        slots[4:6, :] = jnp.concatenate(
            [ids[pl.ds(h, 2, stride=8), :][:, : row.shape[1]] for h in range(8)], 1
        )
        kinds[4:6, :] = jnp.concatenate(
            [top_op[pl.ds(h, 2, stride=8), :] + OPSP * (h % 4) for h in range(8)], 1
        )
        far_row = iota((2 * PAN, 2 * PAN), 0)
        top_row = iota((4 * PAN, 2 * PAN), 0)
        for g in range(6):
            if g < 4:
                hot = (far_row == slots[g : g + 1, :]).astype(f32).astype(bf16)
                table = turned[: RHS * EQ, : 2 * PAN]
            else:
                hot = (top_row == slots[g : g + 1, :]).astype(f32).astype(bf16)
                table = turned[: RHS * EQ, 2 * PAN :]
            picked[g] = nn(table, hot).astype(bf16)

        def build(g, half, per, base):
            ids = kinds[pl.ds(g, 1), :][:, PAN * half : PAN * (half + 1)]
            kind = jnp.broadcast_to(ids, (PAN, PAN)).T
            src = picked[g, :, PAN * half : PAN * (half + 1)]
            for h in range(0, per, 2):
                hot = jnp.concatenate(
                    [
                        (kind == iota((PAN, PAN), 1) + (PAN * t + h * OPSP)).astype(f32).astype(bf16)
                        for t in range(6)
                    ],
                    1,
                )
                y = nn(src, hot)
                for r in range(RHS):
                    for u in range(2):
                        at = pl.multiple_of((base + r * LEAF + h + u) * EQ, 8)
                        for t in range(3):
                            spread[t][pl.ds(at, EQ), :] = y[
                                r * EQ : (r + 1) * EQ, PAN * (t + 3 * u) : PAN * (t + 3 * u + 1)
                            ]

        def far_group(g, carry):
            build(g, 0, 2, g * 4)
            build(g, 1, 2, g * 4 + 2)
            return carry

        def top_group(g, carry):
            build(g, 0, 4, ROWS + (g - 4) * 8)
            build(g, 1, 4, ROWS + (g - 4) * 8 + 4)
            return carry

        lax.fori_loop(0, 4, far_group, 0)
        lax.fori_loop(4, 6, top_group, 0)

    def move(to):
        for h, ops in enumerate((ops0, ops1)):
            rows = ops.shape[0] * 8
            for g in range(FB // 8):
                at = slice(g * 8 * EQ + h * rows, g * 8 * EQ + (h + 1) * rows)
                part = ops[:, 8 * g : 8 * g + 8, :].astype(f32).reshape(rows, ops.shape[2])
                for t in range(2):
                    to[t][at, :] = part[:, PAN * t : PAN * (t + 1)]
                to[2][at, :tail] = part[:, 2 * PAN :]

    def multiply(width, of):
        base = (step - 1) * FB
        left = []
        right = []
        for i in range(width):
            for t in range(3):
                left.append(spread[t][pl.ds(base + i, 2 * ROWS, stride=EQ), :].astype(bf16))
                right.append(of[t][pl.ds(i // 8 * 8 * EQ + i % 8, EQ, stride=8), :].astype(bf16))
        acc[...] += nt(jnp.concatenate(right, 1), jnp.concatenate(left, 1))

    last = pl.num_programs(0) - 1

    @pl.when(step == 0)
    def _():
        move(even)

    @pl.when((step > 0) & (step < last) & (step % 2 == 1))
    def _():
        multiply(FB, even)
        move(odd)

    @pl.when((step > 0) & (step < last) & (step % 2 == 0))
    def _():
        multiply(FB, odd)
        move(even)

    @pl.when(step == last)
    def _():
        multiply(EQ % FB, odd)
        res = acc[...].T
        far = res[:ROWS]
        top = res[ROWS:].astype(bf16)
        row = iota((ROWS, ROWS), 0)
        lane = iota((ROWS, ROWS), 1)
        parent = jnp.zeros((ROWS, ROWS), i32)
        for n in range(LEAF):
            parent = jnp.where(row % LEAF == n, par[0, n], parent)
        hit = (parent == lane % LEAF) & (row // LEAF == lane // LEAF)
        chosen = nn(hit.astype(f32).astype(bf16), top).astype(bf16)
        leaf_row = iota((ROWS, EQ), 0) % LEAF
        down = jnp.zeros((ROWS, EQ), f32)
        for n in range(LEAF):
            down = jnp.where(leaf_row == n, nt(chosen, l2l[octs[0, n]]), down)
        local = (down + far).astype(bf16)
        leaf_row = iota((ROWS, PAN), 0) % LEAF
        res = jnp.zeros((ROWS, PAN), f32)
        for n in range(LEAF):
            res = jnp.where(leaf_row == n, nn(local, tp[n]), res)
        out[...] = res + near_part[...]


def finish(par, octs, far_count, top_count, far_slot, far_op, top_src, top_op, arrived, tables, l2l, tp, near_part):
    chunks = pl.cdiv(EQ, FB)
    half = (EQ // 2, FB, tables.shape[2])
    return pl.pallas_call(
        finish_kernel,
        grid=(chunks + 1,),
        in_specs=[
            SM,
            SM,
            SM,
            SM,
            whole(far_slot),
            whole(far_op),
            whole(top_src),
            whole(top_op),
            whole(arrived),
            pl.BlockSpec(half, lambda i: (0, jnp.minimum(i, chunks - 1), 0)),
            pl.BlockSpec(half, lambda i: (1, jnp.minimum(i, chunks - 1), 0)),
            whole(l2l),
            whole(tp),
            whole(near_part),
        ],
        out_specs=pl.BlockSpec((ROWS, PAN), lambda i: (0, 0)),
        out_shape=jax.ShapeDtypeStruct((ROWS, PAN), f32),
        scratch_shapes=[
            pltpu.VMEM((LEAF, 64), i32),
            pltpu.VMEM((8, 2 * PAN), i32),
            pltpu.VMEM((8, 2 * PAN), i32),
            pltpu.VMEM((BOX, 6 * PAN), bf16),
            pltpu.VMEM((6, RHS * EQ, 2 * PAN), bf16),
            pltpu.VMEM((2 * ROWS * EQ, PAN), f32),
            pltpu.VMEM((2 * ROWS * EQ, PAN), f32),
            pltpu.VMEM((2 * ROWS * EQ, PAN), f32),
            pltpu.VMEM((EQ * FB, PAN), f32),
            pltpu.VMEM((EQ * FB, PAN), f32),
            pltpu.VMEM((EQ * FB, PAN), f32),
            pltpu.VMEM((EQ * FB, PAN), f32),
            pltpu.VMEM((EQ * FB, PAN), f32),
            pltpu.VMEM((EQ * FB, PAN), f32),
            pltpu.VMEM((EQ, 2 * ROWS), f32),
        ],
        compiler_params=pltpu.CompilerParams(vmem_limit_bytes=BIG),
        name="finish",
    )(par, octs, far_count, top_count, far_slot, far_op, top_src, top_op, arrived, tables, tables, l2l, tp, near_part)


def per_device(
    density,
    centres,
    normal,
    to_multipole,
    to_panels,
    m2m_ops,
    l2l_ops,
    m2l_ops,
    near_index,
    near_count,
    send_box,
    send_count,
    far_slot,
    far_op,
    far_count,
    parent_of,
    octant,
    top_src,
    top_op,
    top_count,
):
    dens = density.reshape(ROWS, PAN)
    mult, own, *others, low, high = upward(
        parent_of, octant, dens, centres, normal, to_multipole, m2m_ops
    )
    subs = lax.axis_size("sub")
    pieces = [own]
    for s, piece in enumerate(others, 1):
        pieces.append(lax.ppermute(piece, "sub", [(i, (i + s) % subs) for i in range(subs)]))

    axes = ("leaf", "sub")
    count = lax.axis_size("leaf") * lax.axis_size("sub")
    forward = [(i, i + 1) for i in range(count - 1)]
    backward = [(i + 1, i) for i in range(count - 1)]
    low = lax.ppermute(low, axes, forward)
    high = lax.ppermute(high, axes, backward)

    outgoing = pack(jnp.transpose(send_box[0]), send_count, mult, pieces, (low, high))
    arrived = lax.all_to_all(
        outgoing.reshape(count, CHUNK, PAN), axes, split_axis=0, concat_axis=0, tiled=True
    )

    near_part = near(near_index, near_count, centres, normal, dens, low, high)

    res = finish(
        parent_of,
        octant,
        far_count,
        top_count,
        far_slot,
        far_op,
        top_src,
        top_op,
        arrived.reshape(count * CHUNK, PAN),
        jnp.transpose(m2l_ops, (1, 2, 0)),
        l2l_ops,
        jnp.transpose(to_panels, (0, 2, 1)),
        near_part,
    )
    return res.reshape(RHS, LEAF, PAN)


def solution(mesh):
    both = ("leaf", "sub")
    return jax.shard_map(
        per_device,
        mesh=mesh,
        in_specs=(
            P(None, both, None),
            P(None, both, None),
            P(None, both, None),
            P(both, None, None),
            P(both, None, None),
            P(),
            P(),
            P(),
            P(both, None),
            P(both),
            P(both, None, None),
            P(both, None),
            P(both, None),
            P(both, None),
            P(both),
            P("leaf", "sub"),
            P("leaf", "sub"),
            P("leaf", None),
            P("leaf", None),
            P("leaf"),
        ),
        out_specs=P(None, both, None),
        check_vma=False,
    )
```

```python
import jax
import jax.numpy as jnp
from jax import lax
from jax.experimental import pallas as pl
from jax.experimental.pallas import tpu as pltpu
from jax.sharding import PartitionSpec as P

f32 = jnp.float32
bf16 = jnp.bfloat16
i32 = jnp.int32

RIM = 4
LEAF = 16
RHS = 4
ROWS = RHS * LEAF
EQ = 152
OPSP = 384
PAN = 128
BOX = 640
PIECES = 5
CHUNK = 32
PITCH = 40
EPS = 0.01
FB = 16
MIB = 1 << 20
BIG = 56 * MIB

SM = pl.BlockSpec(memory_space=pltpu.SMEM)


def nt(a, b, **kw):
    return lax.dot_general(a, b, (((1,), (1,)), ((), ())), preferred_element_type=f32, **kw)


def nn(a, b, **kw):
    return lax.dot_general(a, b, (((1,), (0,)), ((), ())), preferred_element_type=f32, **kw)


def whole(x):
    return pl.BlockSpec(x.shape, lambda i: (0,) * len(x.shape))


def iota(shape, dim):
    return lax.broadcasted_iota(i32, shape, dim)


def upward_kernel(par, octs, dens, cen, nrm, tm, m2m, mult_out, c0, x1, c2, x3, cross):
    d = dens[...].astype(bf16)
    leaf_row = iota((ROWS, EQ), 0) % LEAF
    mult = jnp.zeros((ROWS, EQ), f32)
    for n in range(LEAF):
        mult = jnp.where(leaf_row == n, nt(d, tm[n]), mult)
    mb = mult.astype(bf16)
    mult_out[...] = mb
    child = jnp.zeros((ROWS, EQ), f32)
    for n in range(LEAF):
        child = jnp.where(leaf_row == n, nt(mb, m2m[octs[0, n]]), child)
    row = iota((ROWS, ROWS), 0)
    lane = iota((ROWS, ROWS), 1)
    parent = jnp.zeros((ROWS, ROWS), i32)
    for n in range(LEAF):
        parent = jnp.where(lane % LEAF == n, par[0, n], parent)
    box = ((row // 16 + lax.axis_index("sub")) % 4) * 4 + row % 4
    hit = (parent == box) & ((row // 4) % 4 == lane // LEAF)
    part = nn(hit.astype(f32), child, precision=lax.Precision.HIGHEST)
    for s, piece in enumerate((c0, x1, c2, x3)):
        piece[:16, :] = part[16 * s : 16 * s + 16]
    first = lax.axis_index("sub") == 0

    def rim(at, ends, starts):
        x1[16 + at : 16 + at + RIM, :PAN] = ends
        x3[16 + at : 16 + at + RIM, :PAN] = starts
        cross[at : at + RIM, :] = jnp.where(first, starts, ends)

    for a in range(3):
        rim(RIM * a, cen[a, LEAF - RIM :, :], cen[a, :RIM, :])
        rim(RIM * (3 + a), nrm[a, LEAF - RIM :, :], nrm[a, :RIM, :])
    for r in range(RHS):
        rim(
            RIM * (6 + r),
            dens[LEAF * (r + 1) - RIM : LEAF * (r + 1), :],
            dens[LEAF * r : LEAF * r + RIM, :],
        )
    for x in (x1, x3):
        x[16:, PAN:] = jnp.zeros((40, EQ - PAN), f32)


def upward(par, octs, dens, cen, nrm, tm, m2m):
    outs = [
        jax.ShapeDtypeStruct((ROWS, EQ), bf16),
    ]
    small = jax.ShapeDtypeStruct((16, EQ), f32)
    large = jax.ShapeDtypeStruct((56, EQ), f32)
    outs += [small, large, small, large, jax.ShapeDtypeStruct((40, PAN), f32)]
    return pl.pallas_call(
        upward_kernel,
        grid=(1,),
        in_specs=[SM, SM] + [whole(x) for x in (dens, cen, nrm, tm, m2m)],
        out_specs=[whole(x) for x in outs],
        out_shape=outs,
        compiler_params=pltpu.CompilerParams(vmem_limit_bytes=BIG),
        name="upward",
    )(par, octs, dens, cen, nrm, tm, m2m)


def pack_kernel(boxes, counts, mult, c0, x1, c2, x3, cross, out, far, const):
    row = iota((EQ, BOX), 0)
    lane = iota((EQ, BOX), 1)
    own = (c0[...] + x1[:16, :]) + (c2[...] + x3[:16, :])
    own = own.astype(bf16).astype(f32)
    mf = mult[...].astype(f32)
    table = jnp.zeros((24, BOX), f32)
    for r in range(RHS):
        both = jnp.concatenate(
            [mf[16 * r : 16 * r + 16], own[4 * r : 4 * r + 4], jnp.zeros((4, EQ), f32)], 0
        )
        place = (lane == row + EQ * r).astype(f32).astype(bf16)
        table = table + nn(both.astype(bf16), place)
    leaf = iota((LEAF, PAN), 0)
    for j in range(2):
        hot = ((boxes[j : j + 1, :] == leaf) & (counts[...] > j)).astype(f32).T
        y = nn(hot.astype(bf16), table[:LEAF].astype(bf16))
        for t in range(PIECES):
            far[pl.ds(PIECES * j + t, PAN, stride=24), :] = y[:, PAN * t : PAN * (t + 1)]
    const[...] = jnp.zeros_like(const)
    for q in range(4):
        for t in range(PIECES):
            at = PIECES * (2 + q) + t
            const[at : at + 1, :] = table[LEAF + q : LEAF + q + 1, PAN * t : PAN * (t + 1)]
    head = const[:16]
    rest = const[16:].astype(bf16)
    is_far = iota((16, PAN), 0) < 2 * PIECES
    for d in range(PAN):
        out[CHUNK * d : CHUNK * d + 16, :] = jnp.where(
            is_far, far[24 * d : 24 * d + 16, :], head
        ).astype(bf16)
        out[CHUNK * d + 16 : CHUNK * (d + 1), :] = rest


def pack(boxes, counts, mult, pieces, later):
    outs = jax.ShapeDtypeStruct((PAN * CHUNK, PAN), bf16)
    return pl.pallas_call(
        pack_kernel,
        grid=(1,),
        in_specs=[whole(x) for x in (boxes, counts, mult, *pieces)]
        + [pl.BlockSpec(memory_space=pl.ANY)] * len(later),
        out_specs=whole(outs),
        out_shape=outs,
        scratch_shapes=[pltpu.VMEM((PAN * 24, PAN), f32), pltpu.VMEM((CHUNK, PAN), f32)],
        compiler_params=pltpu.CompilerParams(vmem_limit_bytes=BIG),
        name="pack",
    )(boxes, counts, mult, *pieces, *later)


SRC = LEAF + 2 * RIM
BATCH = 4
FEAT = 48
ORDERS = ((0, 0), (0, 1), (1, 0), (0, 2), (1, 1), (2, 0))


def three(x):
    a = x.astype(bf16).astype(f32)
    b = (x - a).astype(bf16).astype(f32)
    c = (x - a - b).astype(bf16).astype(f32)
    return a, b, c


def near_kernel(index, count, cen, nrm, dens, x1, x3, cross, out, raw, fsrc, ftar, fs, dpar, dwide, ft, sums, dist):
    place = lax.axis_index("sub")
    last = lax.axis_size("sub") - 1
    for q in range(10):
        far_side = cross[4 * q : 4 * q + 4, :]
        at = 16 + 4 * q
        raw[q, 0:RIM, :] = jnp.where(place == 0, far_side, x1[at : at + RIM, :PAN])
        raw[q, RIM + LEAF : SRC, :] = jnp.where(place == last, far_side, x3[at : at + RIM, :PAN])
        if q < 3:
            body = cen[q]
        elif q < 6:
            body = nrm[q - 3]
        else:
            body = dens[LEAF * (q - 6) : LEAF * (q - 5), :]
        raw[q, RIM : RIM + LEAF, :] = body
    xs = [raw[a] - 0.5 for a in range(3)]
    ns = [raw[3 + a] for a in range(3)]
    xt = [cen[a] - 0.5 for a in range(3)]
    xs3 = [three(v) for v in xs]
    ns3 = [three(v) for v in ns]
    xt3 = [three(v) for v in xt]
    ss = three(xs[0] * xs[0] + xs[1] * xs[1] + xs[2] * xs[2] + EPS)
    sn = three(xs[0] * ns[0] + xs[1] * ns[1] + xs[2] * ns[2])
    tt = three(xt[0] * xt[0] + xt[1] * xt[1] + xt[2] * xt[2])
    one_s = jnp.ones((SRC, PAN), f32)
    zero_s = jnp.zeros((SRC, PAN), f32)
    one = jnp.ones((LEAF, PAN), f32)
    zero = jnp.zeros((LEAF, PAN), f32)
    feats = []
    for a in range(3):
        for i, j in ORDERS:
            feats.append((xs3[a][i], -2.0 * xt3[a][j], zero))
            feats.append((ns3[a][i], zero, xt3[a][j]))
    for i in range(3):
        feats.append((ss[i], one, zero))
        feats.append((sn[i], zero, -one))
        feats.append((one_s, tt[i], zero))
    while len(feats) < FEAT:
        feats.append((zero_s, zero, zero))
    for k, (s, t1, t2) in enumerate(feats):
        fsrc[k * SRC : (k + 1) * SRC, :] = s
        ftar[0, k * LEAF : (k + 1) * LEAF, :] = t1
        ftar[1, k * LEAF : (k + 1) * LEAF, :] = t2
    for m in range(SRC):
        fs[m] = fsrc[pl.ds(m, FEAT, stride=SRC), :].T.astype(bf16)
    dcols = iota((16, RHS * PAN), 1) // PAN
    pick_r = (iota((16, RHS * PAN), 0) // 3 == dcols).astype(f32).astype(bf16)
    for r in range(RHS):
        for j, part in enumerate(three(raw[6 + r])):
            dpar[pl.ds(3 * r + j, SRC, stride=16), :] = part
            dpar[pl.ds(12 + j, SRC, stride=16), :] = zero_s
    dpar[pl.ds(15, SRC, stride=16), :] = zero_s
    for m in range(SRC):
        wide = nn(dpar[16 * m : 16 * m + 16, :].T.astype(bf16), pick_r)
        for r in range(RHS):
            dwide[m, r] = wide[:, PAN * r : PAN * (r + 1)]
    dwide[SRC] = jnp.zeros((RHS, PAN, PAN), f32)
    for n in range(LEAF):
        ft[n] = jnp.concatenate(
            [ftar[0, pl.ds(n, FEAT, stride=LEAF), :], ftar[1, pl.ds(n, FEAT, stride=LEAF), :]], 1
        ).astype(bf16)
    sums[...] = jnp.zeros_like(sums)
    dist[:, :, :PAN] = jnp.ones((BATCH, 2 * PAN, PAN), f32)
    dist[:, :, PAN:] = jnp.zeros((BATCH, 2 * PAN, PAN), f32)
    pairs = 0
    for n in range(LEAF):
        pairs = pairs + (count[n] + 1) // 2
    steps = (pairs + BATCH - 1) // BATCH + 1

    def step(_, carry):
        n, i = carry[0], carry[1]
        old = carry[2:]
        for u in range(BATCH):
            n1, p1, q1 = old[3 * u], old[3 * u + 1], old[3 * u + 2]
            inv = lax.rsqrt(dist[u, :, :PAN])
            k = dist[u, :, PAN:] * (inv * inv * inv)
            for r in range(RHS):
                term = k[:PAN] * dwide[p1, r] + k[PAN:] * dwide[q1, r]
                sums[n1, r] += jnp.sum(term.reshape(PAN // 8, 8, PAN), 0)
        fresh = []
        for u in range(BATCH):
            at = jnp.minimum(n, LEAF - 1)
            first = 2 * i
            live1 = n < LEAF
            live2 = live1 & (first + 1 < count[at])
            p = index[at, first]
            q = index[at, jnp.minimum(first + 1, index.shape[1] - 1)]
            dist[u] = nn(jnp.concatenate([fs[p], fs[q]], 0), ft[at])
            fresh += [at, jnp.where(live1, p, SRC), jnp.where(live2, q, SRC)]
            more = live1 & (first + 2 < count[at])
            n = jnp.where(more, n, n + 1)
            i = jnp.where(more, i + 1, 0)
        return (n, i) + tuple(fresh)

    start = [jnp.int32(0), jnp.int32(0)] + [jnp.int32(0), jnp.int32(SRC), jnp.int32(SRC)] * BATCH
    lax.fori_loop(0, steps, step, tuple(start))
    for r in range(RHS):
        out[LEAF * r : LEAF * (r + 1), :] = jnp.sum(sums[:, r], 1)


def near(index, count, cen, nrm, dens, x1, x3, cross):
    outs = jax.ShapeDtypeStruct((ROWS, PAN), f32)
    return pl.pallas_call(
        near_kernel,
        grid=(1,),
        in_specs=[SM, SM] + [whole(x) for x in (cen, nrm, dens, x1, x3, cross)],
        out_specs=whole(outs),
        out_shape=outs,
        scratch_shapes=[
            pltpu.VMEM((10, SRC, PAN), f32),
            pltpu.VMEM((FEAT * SRC, PAN), f32),
            pltpu.VMEM((2, FEAT * LEAF, PAN), f32),
            pltpu.VMEM((SRC, PAN, FEAT), bf16),
            pltpu.VMEM((SRC * 16, PAN), f32),
            pltpu.VMEM((SRC + 1, RHS, PAN, PAN), f32),
            pltpu.VMEM((LEAF, FEAT, 2 * PAN), bf16),
            pltpu.VMEM((LEAF, RHS, 8, PAN), f32),
            pltpu.VMEM((BATCH, 2 * PAN, 2 * PAN), f32),
        ],
        compiler_params=pltpu.CompilerParams(vmem_limit_bytes=BIG),
        cost_estimate=pl.CostEstimate(
            flops=20_000_000_00, bytes_accessed=1_000_000, transcendentals=3_600_000
        ),
        name="near",
    )(index, count, cen, nrm, dens, x1, x3, cross)


def finish_kernel(
    par, octs, far_count, top_count, far_slot, far_op, top_src, top_op, arrived, ops0, ops1, l2l_hbm, tp_hbm, near_part, out,
    ids, slots, kinds, turned, picked, s0, s1, s2, m0, m1, m2, m3, m4, m5, acc, l2l, tp, sems,
):
    step = pl.program_id(0)
    spread = (s0, s1, s2)
    late = (
        pltpu.make_async_copy(l2l_hbm, l2l, sems.at[0]),
        pltpu.make_async_copy(tp_hbm, tp, sems.at[1]),
    )
    even = (m0, m1, m2)
    odd = (m3, m4, m5)
    tail = ops0.shape[2] - 2 * PAN

    @pl.when(step == 0)
    def _():
        for copy in late:
            copy.start()
        acc[...] = jnp.zeros_like(acc)
        m2[...] = jnp.zeros_like(m2)
        m5[...] = jnp.zeros_like(m5)
        for p in range(PAN):
            s0[PITCH * p : PITCH * p + CHUNK, :] = arrived[CHUNK * p : CHUNK * (p + 1), :].astype(f32)
        for j in range(6):
            for t in range(PIECES):
                piece = s0[pl.ds(PIECES * j + t, PAN, stride=PITCH), :].T
                turned[PAN * t : PAN * (t + 1), PAN * j : PAN * (j + 1)] = piece.astype(bf16)

        row = iota((LEAF, far_slot.shape[1]), 0)
        lane = iota((LEAF, far_slot.shape[1]), 1)
        live = jnp.zeros(row.shape, i32)
        for n in range(LEAF):
            live = jnp.where(row == n, far_count[n], live)
        slot = far_slot[...]
        ids[...] = jnp.where(lane < live, (slot % 2) * PAN + slot // 2, -1)
        slots[0:4, :] = jnp.concatenate([ids[pl.ds(h, 4, stride=4), :] for h in range(4)], 1)
        kinds[0:4, :] = jnp.concatenate(
            [far_op[pl.ds(h, 4, stride=4), :] + OPSP * (h % 2) for h in range(4)], 1
        )
        row = iota((LEAF, top_src.shape[1]), 0)
        lane = iota((LEAF, top_src.shape[1]), 1)
        live = jnp.zeros(row.shape, i32)
        for n in range(LEAF):
            live = jnp.where(row == n, top_count[n], live)
        slot = top_src[...]
        ids[:, : row.shape[1]] = jnp.where(lane < live, (slot % 4) * PAN + slot // 4, -1)
        slots[4:6, :] = jnp.concatenate(
            [ids[pl.ds(h, 2, stride=8), :][:, : row.shape[1]] for h in range(8)], 1
        )
        kinds[4:6, :] = jnp.concatenate(
            [top_op[pl.ds(h, 2, stride=8), :] + OPSP * (h % 4) for h in range(8)], 1
        )
        far_row = iota((2 * PAN, 2 * PAN), 0)
        top_row = iota((4 * PAN, 2 * PAN), 0)
        for g in range(6):
            if g < 4:
                hot = (far_row == slots[g : g + 1, :]).astype(f32).astype(bf16)
                table = turned[: RHS * EQ, : 2 * PAN]
            else:
                hot = (top_row == slots[g : g + 1, :]).astype(f32).astype(bf16)
                table = turned[: RHS * EQ, 2 * PAN :]
            picked[g] = nn(table, hot).astype(bf16)

        def build(g, half, per, base):
            ids = kinds[pl.ds(g, 1), :][:, PAN * half : PAN * (half + 1)]
            kind = jnp.broadcast_to(ids, (PAN, PAN)).T
            src = picked[g, :, PAN * half : PAN * (half + 1)]
            for h in range(0, per, 2):
                hot = jnp.concatenate(
                    [
                        (kind == iota((PAN, PAN), 1) + (PAN * t + h * OPSP)).astype(f32).astype(bf16)
                        for t in range(6)
                    ],
                    1,
                )
                y = nn(src, hot)
                for r in range(RHS):
                    for u in range(2):
                        at = pl.multiple_of((base + r * LEAF + h + u) * EQ, 8)
                        for t in range(3):
                            spread[t][pl.ds(at, EQ), :] = y[
                                r * EQ : (r + 1) * EQ, PAN * (t + 3 * u) : PAN * (t + 3 * u + 1)
                            ]

        def far_group(g, carry):
            build(g, 0, 2, g * 4)
            build(g, 1, 2, g * 4 + 2)
            return carry

        def top_group(g, carry):
            build(g, 0, 4, ROWS + (g - 4) * 8)
            build(g, 1, 4, ROWS + (g - 4) * 8 + 4)
            return carry

        lax.fori_loop(0, 4, far_group, 0)
        lax.fori_loop(4, 6, top_group, 0)

    def move(to):
        for h, ops in enumerate((ops0, ops1)):
            rows = ops.shape[0] * 8
            for g in range(FB // 8):
                at = slice(g * 8 * EQ + h * rows, g * 8 * EQ + (h + 1) * rows)
                part = ops[:, 8 * g : 8 * g + 8, :].astype(f32).reshape(rows, ops.shape[2])
                for t in range(2):
                    to[t][at, :] = part[:, PAN * t : PAN * (t + 1)]
                to[2][at, :tail] = part[:, 2 * PAN :]

    def multiply(width, of):
        base = (step - 1) * FB
        left = []
        right = []
        for i in range(width):
            for t in range(3):
                left.append(spread[t][pl.ds(base + i, 2 * ROWS, stride=EQ), :].astype(bf16))
                right.append(of[t][pl.ds(i // 8 * 8 * EQ + i % 8, EQ, stride=8), :].astype(bf16))
        acc[...] += nt(jnp.concatenate(right, 1), jnp.concatenate(left, 1))

    last = pl.num_programs(0) - 1

    @pl.when(step == 0)
    def _():
        move(even)

    @pl.when((step > 0) & (step < last) & (step % 2 == 1))
    def _():
        multiply(FB, even)
        move(odd)

    @pl.when((step > 0) & (step < last) & (step % 2 == 0))
    def _():
        multiply(FB, odd)
        move(even)

    @pl.when(step == last)
    def _():
        multiply(EQ % FB, odd)
        for copy in late:
            copy.wait()
        res = acc[...].T
        far = res[:ROWS]
        top = res[ROWS:].astype(bf16)
        row = iota((ROWS, ROWS), 0)
        lane = iota((ROWS, ROWS), 1)
        parent = jnp.zeros((ROWS, ROWS), i32)
        for n in range(LEAF):
            parent = jnp.where(row % LEAF == n, par[0, n], parent)
        hit = (parent == lane % LEAF) & (row // LEAF == lane // LEAF)
        chosen = nn(hit.astype(f32).astype(bf16), top).astype(bf16)
        leaf_row = iota((ROWS, EQ), 0) % LEAF
        down = jnp.zeros((ROWS, EQ), f32)
        for n in range(LEAF):
            down = jnp.where(leaf_row == n, nt(chosen, l2l[octs[0, n]]), down)
        local = (down + far).astype(bf16)
        leaf_row = iota((ROWS, PAN), 0) % LEAF
        res = jnp.zeros((ROWS, PAN), f32)
        for n in range(LEAF):
            res = jnp.where(leaf_row == n, nn(local, tp[n]), res)
        out[...] = res + near_part[...]


def finish(par, octs, far_count, top_count, far_slot, far_op, top_src, top_op, arrived, tables, l2l, tp, near_part):
    chunks = pl.cdiv(EQ, FB)
    half = (EQ // 2, FB, tables.shape[2])
    return pl.pallas_call(
        finish_kernel,
        grid=(chunks + 1,),
        in_specs=[
            SM,
            SM,
            SM,
            SM,
            whole(far_slot),
            whole(far_op),
            whole(top_src),
            whole(top_op),
            whole(arrived),
            pl.BlockSpec(half, lambda i: (0, jnp.minimum(i, chunks - 1), 0)),
            pl.BlockSpec(half, lambda i: (1, jnp.minimum(i, chunks - 1), 0)),
            pl.BlockSpec(memory_space=pl.ANY),
            pl.BlockSpec(memory_space=pl.ANY),
            whole(near_part),
        ],
        out_specs=pl.BlockSpec((ROWS, PAN), lambda i: (0, 0)),
        out_shape=jax.ShapeDtypeStruct((ROWS, PAN), f32),
        scratch_shapes=[
            pltpu.VMEM((LEAF, 64), i32),
            pltpu.VMEM((8, 2 * PAN), i32),
            pltpu.VMEM((8, 2 * PAN), i32),
            pltpu.VMEM((BOX, 6 * PAN), bf16),
            pltpu.VMEM((6, RHS * EQ, 2 * PAN), bf16),
            pltpu.VMEM((2 * ROWS * EQ, PAN), f32),
            pltpu.VMEM((2 * ROWS * EQ, PAN), f32),
            pltpu.VMEM((2 * ROWS * EQ, PAN), f32),
            pltpu.VMEM((EQ * FB, PAN), f32),
            pltpu.VMEM((EQ * FB, PAN), f32),
            pltpu.VMEM((EQ * FB, PAN), f32),
            pltpu.VMEM((EQ * FB, PAN), f32),
            pltpu.VMEM((EQ * FB, PAN), f32),
            pltpu.VMEM((EQ * FB, PAN), f32),
            pltpu.VMEM((EQ, 2 * ROWS), f32),
            pltpu.VMEM(l2l.shape, bf16),
            pltpu.VMEM(tp.shape, bf16),
            pltpu.SemaphoreType.DMA((2,)),
        ],
        compiler_params=pltpu.CompilerParams(vmem_limit_bytes=BIG),
        name="finish",
    )(par, octs, far_count, top_count, far_slot, far_op, top_src, top_op, arrived, tables, tables, l2l, tp, near_part)


def per_device(
    density,
    centres,
    normal,
    to_multipole,
    to_panels,
    m2m_ops,
    l2l_ops,
    m2l_ops,
    near_index,
    near_count,
    send_box,
    send_count,
    far_slot,
    far_op,
    far_count,
    parent_of,
    octant,
    top_src,
    top_op,
    top_count,
):
    dens = density.reshape(ROWS, PAN)
    mult, own, *others, cross = upward(
        parent_of, octant, dens, centres, normal, to_multipole, m2m_ops
    )
    axes = ("leaf", "sub")
    subs = lax.axis_size("sub")
    count = lax.axis_size("leaf") * subs
    pieces = [own]
    for s, piece in enumerate(others, 1):
        pieces.append(lax.ppermute(piece, "sub", [(i, (i + s) % subs) for i in range(subs)]))
    ends = range(subs - 1, count - 1, subs)
    cross = lax.ppermute(cross, axes, [(i, i + 1) for i in ends] + [(i + 1, i) for i in ends])

    outgoing = pack(jnp.transpose(send_box[0]), send_count, mult, pieces, (cross,))
    arrived = lax.all_to_all(
        outgoing.reshape(count, CHUNK, PAN), axes, split_axis=0, concat_axis=0, tiled=True
    )

    near_part = near(near_index, near_count, centres, normal, dens, pieces[1], pieces[3], cross)

    res = finish(
        parent_of,
        octant,
        far_count,
        top_count,
        far_slot,
        far_op,
        top_src,
        top_op,
        arrived.reshape(count * CHUNK, PAN),
        jnp.transpose(m2l_ops, (1, 2, 0)),
        l2l_ops,
        jnp.transpose(to_panels, (0, 2, 1)),
        near_part,
    )
    return res.reshape(RHS, LEAF, PAN)


def solution(mesh):
    both = ("leaf", "sub")
    return jax.shard_map(
        per_device,
        mesh=mesh,
        in_specs=(
            P(None, both, None),
            P(None, both, None),
            P(None, both, None),
            P(both, None, None),
            P(both, None, None),
            P(),
            P(),
            P(),
            P(both, None),
            P(both),
            P(both, None, None),
            P(both, None),
            P(both, None),
            P(both, None),
            P(both),
            P("leaf", "sub"),
            P("leaf", "sub"),
            P("leaf", None),
            P("leaf", None),
            P("leaf"),
        ),
        out_specs=P(None, both, None),
        check_vma=False,
    )
```

```python
import jax
import jax.numpy as jnp
from jax import lax
from jax.experimental import pallas as pl
from jax.experimental.pallas import tpu as pltpu
from jax.sharding import PartitionSpec as P

f32 = jnp.float32
bf16 = jnp.bfloat16
i32 = jnp.int32

RIM = 4
LEAF = 16
RHS = 4
ROWS = RHS * LEAF
EQ = 152
OPSP = 384
PAN = 128
BOX = 640
PIECES = 5
CHUNK = 32
PITCH = 40
EPS = 0.01
FB = 16
MIB = 1 << 20
BIG = 64 * MIB

SM = pl.BlockSpec(memory_space=pltpu.SMEM)


def nt(a, b, **kw):
    return lax.dot_general(a, b, (((1,), (1,)), ((), ())), preferred_element_type=f32, **kw)


def nn(a, b, **kw):
    return lax.dot_general(a, b, (((1,), (0,)), ((), ())), preferred_element_type=f32, **kw)


def whole(x):
    return pl.BlockSpec(x.shape, lambda i: (0,) * len(x.shape))


def iota(shape, dim):
    return lax.broadcasted_iota(i32, shape, dim)


def upward_kernel(par, octs, dens, cen, nrm, tm, m2m, mult_out, c0, x1, c2, x3, cross):
    d = dens[...].astype(bf16)
    leaf_row = iota((ROWS, EQ), 0) % LEAF
    mult = jnp.zeros((ROWS, EQ), f32)
    for n in range(LEAF):
        mult = jnp.where(leaf_row == n, nt(d, tm[n]), mult)
    mb = mult.astype(bf16)
    mult_out[...] = mb
    child = jnp.zeros((ROWS, EQ), f32)
    for n in range(LEAF):
        child = jnp.where(leaf_row == n, nt(mb, m2m[octs[0, n]]), child)
    row = iota((ROWS, ROWS), 0)
    lane = iota((ROWS, ROWS), 1)
    parent = jnp.zeros((ROWS, ROWS), i32)
    for n in range(LEAF):
        parent = jnp.where(lane % LEAF == n, par[0, n], parent)
    box = ((row // 16 + lax.axis_index("sub")) % 4) * 4 + row % 4
    hit = (parent == box) & ((row // 4) % 4 == lane // LEAF)
    part = nn(hit.astype(f32), child, precision=lax.Precision.HIGHEST)
    for s, piece in enumerate((c0, x1, c2, x3)):
        piece[:16, :] = part[16 * s : 16 * s + 16]
    first = lax.axis_index("sub") == 0

    def rim(at, ends, starts):
        x1[16 + at : 16 + at + RIM, :PAN] = ends
        x3[16 + at : 16 + at + RIM, :PAN] = starts
        cross[at : at + RIM, :] = jnp.where(first, starts, ends)

    for a in range(3):
        rim(RIM * a, cen[a, LEAF - RIM :, :], cen[a, :RIM, :])
        rim(RIM * (3 + a), nrm[a, LEAF - RIM :, :], nrm[a, :RIM, :])
    for r in range(RHS):
        rim(
            RIM * (6 + r),
            dens[LEAF * (r + 1) - RIM : LEAF * (r + 1), :],
            dens[LEAF * r : LEAF * r + RIM, :],
        )
    for x in (x1, x3):
        x[16:, PAN:] = jnp.zeros((40, EQ - PAN), f32)


def upward(par, octs, dens, cen, nrm, tm, m2m):
    outs = [
        jax.ShapeDtypeStruct((ROWS, EQ), bf16),
    ]
    small = jax.ShapeDtypeStruct((16, EQ), f32)
    large = jax.ShapeDtypeStruct((56, EQ), f32)
    outs += [small, large, small, large, jax.ShapeDtypeStruct((40, PAN), f32)]
    return pl.pallas_call(
        upward_kernel,
        grid=(1,),
        in_specs=[SM, SM] + [whole(x) for x in (dens, cen, nrm, tm, m2m)],
        out_specs=[whole(x) for x in outs],
        out_shape=outs,
        compiler_params=pltpu.CompilerParams(vmem_limit_bytes=BIG),
        name="upward",
    )(par, octs, dens, cen, nrm, tm, m2m)


def pack_kernel(boxes, counts, mult, c0, x1, c2, x3, cross, out, far, const):
    row = iota((EQ, BOX), 0)
    lane = iota((EQ, BOX), 1)
    own = (c0[...] + x1[:16, :]) + (c2[...] + x3[:16, :])
    own = own.astype(bf16).astype(f32)
    mf = mult[...].astype(f32)
    table = jnp.zeros((24, BOX), f32)
    for r in range(RHS):
        both = jnp.concatenate(
            [mf[16 * r : 16 * r + 16], own[4 * r : 4 * r + 4], jnp.zeros((4, EQ), f32)], 0
        )
        place = (lane == row + EQ * r).astype(f32).astype(bf16)
        table = table + nn(both.astype(bf16), place)
    leaf = iota((LEAF, PAN), 0)
    for j in range(2):
        hot = ((boxes[j : j + 1, :] == leaf) & (counts[...] > j)).astype(f32).T
        y = nn(hot.astype(bf16), table[:LEAF].astype(bf16))
        for t in range(PIECES):
            far[pl.ds(PIECES * j + t, PAN, stride=24), :] = y[:, PAN * t : PAN * (t + 1)]
    const[...] = jnp.zeros_like(const)
    for q in range(4):
        for t in range(PIECES):
            at = PIECES * (2 + q) + t
            const[at : at + 1, :] = table[LEAF + q : LEAF + q + 1, PAN * t : PAN * (t + 1)]
    head = const[:16]
    rest = const[16:].astype(bf16)
    is_far = iota((16, PAN), 0) < 2 * PIECES
    for d in range(PAN):
        out[CHUNK * d : CHUNK * d + 16, :] = jnp.where(
            is_far, far[24 * d : 24 * d + 16, :], head
        ).astype(bf16)
        out[CHUNK * d + 16 : CHUNK * (d + 1), :] = rest


def pack(boxes, counts, mult, pieces, later):
    outs = jax.ShapeDtypeStruct((PAN * CHUNK, PAN), bf16)
    return pl.pallas_call(
        pack_kernel,
        grid=(1,),
        in_specs=[whole(x) for x in (boxes, counts, mult, *pieces)]
        + [pl.BlockSpec(memory_space=pl.ANY)] * len(later),
        out_specs=whole(outs),
        out_shape=outs,
        scratch_shapes=[pltpu.VMEM((PAN * 24, PAN), f32), pltpu.VMEM((CHUNK, PAN), f32)],
        compiler_params=pltpu.CompilerParams(vmem_limit_bytes=BIG),
        name="pack",
    )(boxes, counts, mult, *pieces, *later)


SRC = LEAF + 2 * RIM
BATCH = 4
FEAT = 48
ORDERS = ((0, 0), (0, 1), (1, 0), (0, 2), (1, 1), (2, 0))


def three(x):
    a = x.astype(bf16).astype(f32)
    b = (x - a).astype(bf16).astype(f32)
    c = (x - a - b).astype(bf16).astype(f32)
    return a, b, c


def near_kernel(index, count, cen, nrm, dens, x1, x3, cross, out, raw, fsrc, ftar, fs, dpar, dwide, ft, sums, dist):
    place = lax.axis_index("sub")
    last = lax.axis_size("sub") - 1
    for q in range(10):
        far_side = cross[4 * q : 4 * q + 4, :]
        at = 16 + 4 * q
        raw[q, 0:RIM, :] = jnp.where(place == 0, far_side, x1[at : at + RIM, :PAN])
        raw[q, RIM + LEAF : SRC, :] = jnp.where(place == last, far_side, x3[at : at + RIM, :PAN])
        if q < 3:
            body = cen[q]
        elif q < 6:
            body = nrm[q - 3]
        else:
            body = dens[LEAF * (q - 6) : LEAF * (q - 5), :]
        raw[q, RIM : RIM + LEAF, :] = body
    xs = [raw[a] - 0.5 for a in range(3)]
    ns = [raw[3 + a] for a in range(3)]
    xt = [cen[a] - 0.5 for a in range(3)]
    xs3 = [three(v) for v in xs]
    ns3 = [three(v) for v in ns]
    xt3 = [three(v) for v in xt]
    ss = three(xs[0] * xs[0] + xs[1] * xs[1] + xs[2] * xs[2] + EPS)
    sn = three(xs[0] * ns[0] + xs[1] * ns[1] + xs[2] * ns[2])
    tt = three(xt[0] * xt[0] + xt[1] * xt[1] + xt[2] * xt[2])
    one_s = jnp.ones((SRC, PAN), f32)
    zero_s = jnp.zeros((SRC, PAN), f32)
    one = jnp.ones((LEAF, PAN), f32)
    zero = jnp.zeros((LEAF, PAN), f32)
    feats = []
    for a in range(3):
        for i, j in ORDERS:
            feats.append((xs3[a][i], -2.0 * xt3[a][j], zero))
            feats.append((ns3[a][i], zero, xt3[a][j]))
    for i in range(3):
        feats.append((ss[i], one, zero))
        feats.append((sn[i], zero, -one))
        feats.append((one_s, tt[i], zero))
    while len(feats) < FEAT:
        feats.append((zero_s, zero, zero))
    for k, (s, t1, t2) in enumerate(feats):
        fsrc[k * SRC : (k + 1) * SRC, :] = s
        ftar[0, k * LEAF : (k + 1) * LEAF, :] = t1
        ftar[1, k * LEAF : (k + 1) * LEAF, :] = t2
    for m in range(SRC):
        fs[m] = fsrc[pl.ds(m, FEAT, stride=SRC), :].T.astype(bf16)
    dcols = iota((16, RHS * PAN), 1) // PAN
    pick_r = (iota((16, RHS * PAN), 0) // 3 == dcols).astype(f32).astype(bf16)
    for r in range(RHS):
        for j, part in enumerate(three(raw[6 + r])):
            dpar[pl.ds(3 * r + j, SRC, stride=16), :] = part
            dpar[pl.ds(12 + j, SRC, stride=16), :] = zero_s
    dpar[pl.ds(15, SRC, stride=16), :] = zero_s
    for m in range(SRC):
        wide = nn(dpar[16 * m : 16 * m + 16, :].T.astype(bf16), pick_r)
        for r in range(RHS):
            dwide[m, r] = wide[:, PAN * r : PAN * (r + 1)]
    dwide[SRC] = jnp.zeros((RHS, PAN, PAN), f32)
    for n in range(LEAF):
        ft[n] = jnp.concatenate(
            [ftar[0, pl.ds(n, FEAT, stride=LEAF), :], ftar[1, pl.ds(n, FEAT, stride=LEAF), :]], 1
        ).astype(bf16)
    sums[...] = jnp.zeros_like(sums)
    dist[:, :, :PAN] = jnp.ones((BATCH, 2 * PAN, PAN), f32)
    dist[:, :, PAN:] = jnp.zeros((BATCH, 2 * PAN, PAN), f32)
    pairs = 0
    for n in range(LEAF):
        pairs = pairs + (count[n] + 1) // 2
    steps = (pairs + BATCH - 1) // BATCH + 1

    def step(_, carry):
        n, i = carry[0], carry[1]
        old = carry[2:]
        for u in range(BATCH):
            n1, p1, q1 = old[3 * u], old[3 * u + 1], old[3 * u + 2]
            inv = lax.rsqrt(dist[u, :, :PAN])
            k = dist[u, :, PAN:] * (inv * inv * inv)
            for r in range(RHS):
                term = k[:PAN] * dwide[p1, r] + k[PAN:] * dwide[q1, r]
                sums[n1, r] += jnp.sum(term.reshape(PAN // 8, 8, PAN), 0)
        fresh = []
        for u in range(BATCH):
            at = jnp.minimum(n, LEAF - 1)
            first = 2 * i
            live1 = n < LEAF
            live2 = live1 & (first + 1 < count[at])
            p = index[at, first]
            q = index[at, jnp.minimum(first + 1, index.shape[1] - 1)]
            dist[u] = nn(jnp.concatenate([fs[p], fs[q]], 0), ft[at])
            fresh += [at, jnp.where(live1, p, SRC), jnp.where(live2, q, SRC)]
            more = live1 & (first + 2 < count[at])
            n = jnp.where(more, n, n + 1)
            i = jnp.where(more, i + 1, 0)
        return (n, i) + tuple(fresh)

    start = [jnp.int32(0), jnp.int32(0)] + [jnp.int32(0), jnp.int32(SRC), jnp.int32(SRC)] * BATCH
    lax.fori_loop(0, steps, step, tuple(start))
    for r in range(RHS):
        out[LEAF * r : LEAF * (r + 1), :] = jnp.sum(sums[:, r], 1)


def near(index, count, cen, nrm, dens, x1, x3, cross):
    outs = jax.ShapeDtypeStruct((ROWS, PAN), f32)
    return pl.pallas_call(
        near_kernel,
        grid=(1,),
        in_specs=[SM, SM] + [whole(x) for x in (cen, nrm, dens, x1, x3, cross)],
        out_specs=whole(outs),
        out_shape=outs,
        scratch_shapes=[
            pltpu.VMEM((10, SRC, PAN), f32),
            pltpu.VMEM((FEAT * SRC, PAN), f32),
            pltpu.VMEM((2, FEAT * LEAF, PAN), f32),
            pltpu.VMEM((SRC, PAN, FEAT), bf16),
            pltpu.VMEM((SRC * 16, PAN), f32),
            pltpu.VMEM((SRC + 1, RHS, PAN, PAN), f32),
            pltpu.VMEM((LEAF, FEAT, 2 * PAN), bf16),
            pltpu.VMEM((LEAF, RHS, 8, PAN), f32),
            pltpu.VMEM((BATCH, 2 * PAN, 2 * PAN), f32),
        ],
        compiler_params=pltpu.CompilerParams(vmem_limit_bytes=BIG),
        cost_estimate=pl.CostEstimate(
            flops=20_000_000_00, bytes_accessed=1_000_000, transcendentals=3_600_000
        ),
        name="near",
    )(index, count, cen, nrm, dens, x1, x3, cross)


def finish_kernel(
    par, octs, far_count, top_count, far_slot, far_op, top_src, top_op, arrived, ops0, ops1, l2l_hbm, tp_hbm, near_part, out,
    ids, slots, kinds, turned, picked, s0, s1, s2, m0, m1, m2, m3, m4, m5, acc, l2l, tp, sems,
):
    step = pl.program_id(0)
    spread = (s0, s1, s2)
    late = (
        pltpu.make_async_copy(l2l_hbm, l2l, sems.at[0]),
        pltpu.make_async_copy(tp_hbm, tp, sems.at[1]),
    )
    even = (m0, m1, m2)
    odd = (m3, m4, m5)
    tail = ops0.shape[2] - 2 * PAN

    @pl.when(step == 0)
    def _():
        for copy in late:
            copy.start()
        acc[...] = jnp.zeros_like(acc)
        m2[...] = jnp.zeros_like(m2)
        m5[...] = jnp.zeros_like(m5)
        for p in range(PAN):
            s0[PITCH * p : PITCH * p + CHUNK, :] = arrived[CHUNK * p : CHUNK * (p + 1), :].astype(f32)
        for j in range(6):
            for t in range(PIECES):
                piece = s0[pl.ds(PIECES * j + t, PAN, stride=PITCH), :].T
                turned[PAN * t : PAN * (t + 1), PAN * j : PAN * (j + 1)] = piece.astype(bf16)

        row = iota((LEAF, far_slot.shape[1]), 0)
        lane = iota((LEAF, far_slot.shape[1]), 1)
        live = jnp.zeros(row.shape, i32)
        for n in range(LEAF):
            live = jnp.where(row == n, far_count[n], live)
        slot = far_slot[...]
        ids[...] = jnp.where(lane < live, (slot % 2) * PAN + slot // 2, -1)
        slots[0:4, :] = jnp.concatenate([ids[pl.ds(h, 4, stride=4), :] for h in range(4)], 1)
        kinds[0:4, :] = jnp.concatenate(
            [far_op[pl.ds(h, 4, stride=4), :] + OPSP * (h % 2) for h in range(4)], 1
        )
        row = iota((LEAF, top_src.shape[1]), 0)
        lane = iota((LEAF, top_src.shape[1]), 1)
        live = jnp.zeros(row.shape, i32)
        for n in range(LEAF):
            live = jnp.where(row == n, top_count[n], live)
        slot = top_src[...]
        ids[:, : row.shape[1]] = jnp.where(lane < live, (slot % 4) * PAN + slot // 4, -1)
        slots[4:6, :] = jnp.concatenate(
            [ids[pl.ds(h, 2, stride=8), :][:, : row.shape[1]] for h in range(8)], 1
        )
        kinds[4:6, :] = jnp.concatenate(
            [top_op[pl.ds(h, 2, stride=8), :] + OPSP * (h % 4) for h in range(8)], 1
        )
        far_row = iota((2 * PAN, 2 * PAN), 0)
        top_row = iota((4 * PAN, 2 * PAN), 0)
        for g in range(6):
            if g < 4:
                hot = (far_row == slots[g : g + 1, :]).astype(f32).astype(bf16)
                table = turned[: RHS * EQ, : 2 * PAN]
            else:
                hot = (top_row == slots[g : g + 1, :]).astype(f32).astype(bf16)
                table = turned[: RHS * EQ, 2 * PAN :]
            picked[g] = nn(table, hot).astype(bf16)

        def build(g, half, per, base):
            ids = kinds[pl.ds(g, 1), :][:, PAN * half : PAN * (half + 1)]
            kind = jnp.broadcast_to(ids, (PAN, PAN)).T
            src = picked[g, :, PAN * half : PAN * (half + 1)]
            for h in range(0, per, 2):
                hot = jnp.concatenate(
                    [
                        (kind == iota((PAN, PAN), 1) + (PAN * t + h * OPSP)).astype(f32).astype(bf16)
                        for t in range(6)
                    ],
                    1,
                )
                y = nn(src, hot)
                for r in range(RHS):
                    for u in range(2):
                        at = pl.multiple_of((base + r * LEAF + h + u) * EQ, 8)
                        for t in range(3):
                            spread[t][pl.ds(at, EQ), :] = y[
                                r * EQ : (r + 1) * EQ, PAN * (t + 3 * u) : PAN * (t + 3 * u + 1)
                            ]

        def far_group(g, carry):
            build(g, 0, 2, g * 4)
            build(g, 1, 2, g * 4 + 2)
            return carry

        def top_group(g, carry):
            build(g, 0, 4, ROWS + (g - 4) * 8)
            build(g, 1, 4, ROWS + (g - 4) * 8 + 4)
            return carry

        lax.fori_loop(0, 4, far_group, 0)
        lax.fori_loop(4, 6, top_group, 0)

    def move(to):
        for h, ops in enumerate((ops0, ops1)):
            rows = ops.shape[0] * 8
            for g in range(FB // 8):
                at = slice(g * 8 * EQ + h * rows, g * 8 * EQ + (h + 1) * rows)
                part = ops[:, 8 * g : 8 * g + 8, :].astype(f32).reshape(rows, ops.shape[2])
                for t in range(2):
                    to[t][at, :] = part[:, PAN * t : PAN * (t + 1)]
                to[2][at, :tail] = part[:, 2 * PAN :]

    def multiply(width, of):
        base = (step - 1) * FB
        left = []
        right = []
        for i in range(width):
            for t in range(3):
                left.append(spread[t][pl.ds(base + i, 2 * ROWS, stride=EQ), :].astype(bf16))
                right.append(of[t][pl.ds(i // 8 * 8 * EQ + i % 8, EQ, stride=8), :].astype(bf16))
        acc[...] += nt(jnp.concatenate(right, 1), jnp.concatenate(left, 1))

    last = pl.num_programs(0) - 1

    @pl.when(step == 0)
    def _():
        move(even)

    @pl.when((step > 0) & (step < last) & (step % 2 == 1))
    def _():
        multiply(FB, even)
        move(odd)

    @pl.when((step > 0) & (step < last) & (step % 2 == 0))
    def _():
        multiply(FB, odd)
        move(even)

    @pl.when(step == last)
    def _():
        multiply(EQ % FB, odd)
        for copy in late:
            copy.wait()
        res = acc[...].T
        far = res[:ROWS]
        top = res[ROWS:].astype(bf16)
        row = iota((ROWS, ROWS), 0)
        lane = iota((ROWS, ROWS), 1)
        parent = jnp.zeros((ROWS, ROWS), i32)
        for n in range(LEAF):
            parent = jnp.where(row % LEAF == n, par[0, n], parent)
        hit = (parent == lane % LEAF) & (row // LEAF == lane // LEAF)
        chosen = nn(hit.astype(f32).astype(bf16), top).astype(bf16)
        leaf_row = iota((ROWS, EQ), 0) % LEAF
        down = jnp.zeros((ROWS, EQ), f32)
        for n in range(LEAF):
            down = jnp.where(leaf_row == n, nt(chosen, l2l[octs[0, n]]), down)
        local = (down + far).astype(bf16)
        leaf_row = iota((ROWS, PAN), 0) % LEAF
        res = jnp.zeros((ROWS, PAN), f32)
        for n in range(LEAF):
            res = jnp.where(leaf_row == n, nn(local, tp[n]), res)
        out[...] = res + near_part[...]


def finish(par, octs, far_count, top_count, far_slot, far_op, top_src, top_op, arrived, tables, l2l, tp, near_part):
    chunks = pl.cdiv(EQ, FB)
    half = (EQ // 2, FB, tables.shape[2])
    return pl.pallas_call(
        finish_kernel,
        grid=(chunks + 1,),
        in_specs=[
            SM,
            SM,
            SM,
            SM,
            whole(far_slot),
            whole(far_op),
            whole(top_src),
            whole(top_op),
            whole(arrived),
            pl.BlockSpec(half, lambda i: (0, jnp.minimum(i, chunks - 1), 0)),
            pl.BlockSpec(half, lambda i: (1, jnp.minimum(i, chunks - 1), 0)),
            pl.BlockSpec(memory_space=pl.ANY),
            pl.BlockSpec(memory_space=pl.ANY),
            whole(near_part),
        ],
        out_specs=pl.BlockSpec((ROWS, PAN), lambda i: (0, 0)),
        out_shape=jax.ShapeDtypeStruct((ROWS, PAN), f32),
        scratch_shapes=[
            pltpu.VMEM((LEAF, 64), i32),
            pltpu.VMEM((8, 2 * PAN), i32),
            pltpu.VMEM((8, 2 * PAN), i32),
            pltpu.VMEM((BOX, 6 * PAN), bf16),
            pltpu.VMEM((6, RHS * EQ, 2 * PAN), bf16),
            pltpu.VMEM((2 * ROWS * EQ, PAN), f32),
            pltpu.VMEM((2 * ROWS * EQ, PAN), f32),
            pltpu.VMEM((2 * ROWS * EQ, PAN), f32),
            pltpu.VMEM((EQ * FB, PAN), f32),
            pltpu.VMEM((EQ * FB, PAN), f32),
            pltpu.VMEM((EQ * FB, PAN), f32),
            pltpu.VMEM((EQ * FB, PAN), f32),
            pltpu.VMEM((EQ * FB, PAN), f32),
            pltpu.VMEM((EQ * FB, PAN), f32),
            pltpu.VMEM((EQ, 2 * ROWS), f32),
            pltpu.VMEM(l2l.shape, bf16),
            pltpu.VMEM(tp.shape, bf16),
            pltpu.SemaphoreType.DMA((2,)),
        ],
        compiler_params=pltpu.CompilerParams(vmem_limit_bytes=BIG),
        name="finish",
    )(par, octs, far_count, top_count, far_slot, far_op, top_src, top_op, arrived, tables, tables, l2l, tp, near_part)


def per_device(
    density,
    centres,
    normal,
    to_multipole,
    to_panels,
    m2m_ops,
    l2l_ops,
    m2l_ops,
    near_index,
    near_count,
    send_box,
    send_count,
    far_slot,
    far_op,
    far_count,
    parent_of,
    octant,
    top_src,
    top_op,
    top_count,
):
    dens = density.reshape(ROWS, PAN)
    mult, own, *others, cross = upward(
        parent_of, octant, dens, centres, normal, to_multipole, m2m_ops
    )
    axes = ("leaf", "sub")
    subs = lax.axis_size("sub")
    count = lax.axis_size("leaf") * subs
    pieces = [own]
    for s, piece in enumerate(others, 1):
        pieces.append(lax.ppermute(piece, "sub", [(i, (i + s) % subs) for i in range(subs)]))
    ends = range(subs - 1, count - 1, subs)
    cross = lax.ppermute(cross, axes, [(i, i + 1) for i in ends] + [(i + 1, i) for i in ends])

    outgoing = pack(jnp.transpose(send_box[0]), send_count, mult, pieces, (cross,))
    arrived = lax.all_to_all(
        outgoing.reshape(count, CHUNK, PAN), axes, split_axis=0, concat_axis=0, tiled=True
    )

    near_part = near(near_index, near_count, centres, normal, dens, pieces[1], pieces[3], cross)

    res = finish(
        parent_of,
        octant,
        far_count,
        top_count,
        far_slot,
        far_op,
        top_src,
        top_op,
        arrived.reshape(count * CHUNK, PAN),
        jnp.transpose(m2l_ops, (1, 2, 0)),
        l2l_ops,
        jnp.transpose(to_panels, (0, 2, 1)),
        near_part,
    )
    return res.reshape(RHS, LEAF, PAN)


def solution(mesh):
    both = ("leaf", "sub")
    return jax.shard_map(
        per_device,
        mesh=mesh,
        in_specs=(
            P(None, both, None),
            P(None, both, None),
            P(None, both, None),
            P(both, None, None),
            P(both, None, None),
            P(),
            P(),
            P(),
            P(both, None),
            P(both),
            P(both, None, None),
            P(both, None),
            P(both, None),
            P(both, None),
            P(both),
            P("leaf", "sub"),
            P("leaf", "sub"),
            P("leaf", None),
            P("leaf", None),
            P("leaf"),
        ),
        out_specs=P(None, both, None),
        check_vma=False,
    )
```

```python
import jax
import jax.numpy as jnp
from jax import lax
from jax.experimental import pallas as pl
from jax.experimental.pallas import tpu as pltpu
from jax.sharding import PartitionSpec as P

f32 = jnp.float32
bf16 = jnp.bfloat16
i32 = jnp.int32

RIM = 4
LEAF = 16
RHS = 4
ROWS = RHS * LEAF
EQ = 152
OPSP = 384
PAN = 128
BOX = 640
PIECES = 5
CHUNK = 32
PITCH = 40
EPS = 0.01
FB = 16
MIB = 1 << 20
BIG = 64 * MIB

SM = pl.BlockSpec(memory_space=pltpu.SMEM)


def nt(a, b, **kw):
    return lax.dot_general(a, b, (((1,), (1,)), ((), ())), preferred_element_type=f32, **kw)


def nn(a, b, **kw):
    return lax.dot_general(a, b, (((1,), (0,)), ((), ())), preferred_element_type=f32, **kw)


def whole(x):
    return pl.BlockSpec(x.shape, lambda i: (0,) * len(x.shape))


def iota(shape, dim):
    return lax.broadcasted_iota(i32, shape, dim)


def upward_kernel(par, octs, dens, cen, nrm, tm, m2m, mult_out, c0, x1, c2, x3, cross):
    d = dens[...].astype(bf16)
    leaf_row = iota((ROWS, EQ), 0) % LEAF
    mult = jnp.zeros((ROWS, EQ), f32)
    for n in range(LEAF):
        mult = jnp.where(leaf_row == n, nt(d, tm[n]), mult)
    mb = mult.astype(bf16)
    mult_out[...] = mb
    child = jnp.zeros((ROWS, EQ), f32)
    for n in range(LEAF):
        child = jnp.where(leaf_row == n, nt(mb, m2m[octs[0, n]]), child)
    row = iota((ROWS, ROWS), 0)
    lane = iota((ROWS, ROWS), 1)
    parent = jnp.zeros((ROWS, ROWS), i32)
    for n in range(LEAF):
        parent = jnp.where(lane % LEAF == n, par[0, n], parent)
    box = ((row // 16 + lax.axis_index("sub")) % 4) * 4 + row % 4
    hit = (parent == box) & ((row // 4) % 4 == lane // LEAF)
    part = nn(hit.astype(f32), child, precision=lax.Precision.HIGHEST)
    for s, piece in enumerate((c0, x1, c2, x3)):
        piece[:16, :] = part[16 * s : 16 * s + 16]
    first = lax.axis_index("sub") == 0

    def rim(at, ends, starts):
        x1[16 + at : 16 + at + RIM, :PAN] = ends
        x3[16 + at : 16 + at + RIM, :PAN] = starts
        cross[at : at + RIM, :] = jnp.where(first, starts, ends)

    for a in range(3):
        rim(RIM * a, cen[a, LEAF - RIM :, :], cen[a, :RIM, :])
        rim(RIM * (3 + a), nrm[a, LEAF - RIM :, :], nrm[a, :RIM, :])
    for r in range(RHS):
        rim(
            RIM * (6 + r),
            dens[LEAF * (r + 1) - RIM : LEAF * (r + 1), :],
            dens[LEAF * r : LEAF * r + RIM, :],
        )
    for x in (x1, x3):
        x[16:, PAN:] = jnp.zeros((40, EQ - PAN), f32)


def upward(par, octs, dens, cen, nrm, tm, m2m):
    outs = [
        jax.ShapeDtypeStruct((ROWS, EQ), bf16),
    ]
    small = jax.ShapeDtypeStruct((16, EQ), f32)
    large = jax.ShapeDtypeStruct((56, EQ), f32)
    outs += [small, large, small, large, jax.ShapeDtypeStruct((40, PAN), f32)]
    return pl.pallas_call(
        upward_kernel,
        grid=(1,),
        in_specs=[SM, SM] + [whole(x) for x in (dens, cen, nrm, tm, m2m)],
        out_specs=[whole(x) for x in outs],
        out_shape=outs,
        compiler_params=pltpu.CompilerParams(vmem_limit_bytes=BIG),
        name="upward",
    )(par, octs, dens, cen, nrm, tm, m2m)


def boxes_of(mats):
    row = iota((EQ, BOX), 0)
    lane = iota((EQ, BOX), 1)
    table = jnp.zeros((mats[0].shape[0], BOX), f32)
    for r, mat in enumerate(mats):
        place = (lane == row + EQ * r).astype(f32).astype(bf16)
        table = table + nn(mat, place)
    return table


def choose_kernel(boxes, counts, mult, out, far):
    mf = mult[...].astype(f32)
    table = boxes_of([mf[LEAF * r : LEAF * (r + 1)].astype(bf16) for r in range(RHS)]).astype(bf16)
    leaf = iota((LEAF, PAN), 0)
    for j in range(2):
        hot = ((boxes[j : j + 1, :] == leaf) & (counts[...] > j)).astype(f32).T
        y = nn(hot.astype(bf16), table)
        for t in range(PIECES):
            far[pl.ds(PIECES * j + t, PAN, stride=24), :] = y[:, PAN * t : PAN * (t + 1)]
    is_far = iota((16, PAN), 0) < 2 * PIECES
    for d in range(PAN):
        out[16 * d : 16 * (d + 1), :] = jnp.where(is_far, far[24 * d : 24 * d + 16, :], 0.0).astype(
            bf16
        )


def choose(boxes, counts, mult):
    outs = jax.ShapeDtypeStruct((PAN * 16, PAN), bf16)
    return pl.pallas_call(
        choose_kernel,
        grid=(1,),
        in_specs=[whole(x) for x in (boxes, counts, mult)],
        out_specs=whole(outs),
        out_shape=outs,
        scratch_shapes=[pltpu.VMEM((PAN * 24, PAN), f32)],
        compiler_params=pltpu.CompilerParams(vmem_limit_bytes=BIG),
        name="choose",
    )(boxes, counts, mult)


def pack_kernel(far, c0, x1, c2, x3, cross, out, const):
    @pl.when(pl.program_id(0) == 0)
    def _():
        own = (c0[...] + x1[:16, :]) + (c2[...] + x3[:16, :])
        own = own.astype(bf16).astype(f32)
        pad = jnp.zeros((4, EQ), f32)
        table = boxes_of(
            [jnp.concatenate([own[4 * r : 4 * r + 4], pad], 0).astype(bf16) for r in range(RHS)]
        )
        const[...] = jnp.zeros_like(const)
        for q in range(4):
            for t in range(PIECES):
                at = PIECES * (2 + q) + t
                const[at : at + 1, :] = table[q : q + 1, PAN * t : PAN * (t + 1)]

    head = const[:16]
    rest = const[16:].astype(bf16)
    for d in range(far.shape[0] // 16):
        out[CHUNK * d : CHUNK * d + 16, :] = (
            far[16 * d : 16 * (d + 1), :].astype(f32) + head
        ).astype(bf16)
        out[CHUNK * d + 16 : CHUNK * (d + 1), :] = rest


def pack(far, pieces, later):
    steps = 2
    return pl.pallas_call(
        pack_kernel,
        grid=(steps,),
        in_specs=[pl.BlockSpec((PAN * 16 // steps, PAN), lambda i: (i, 0))]
        + [whole(x) for x in pieces]
        + [pl.BlockSpec(memory_space=pl.ANY)] * len(later),
        out_specs=pl.BlockSpec((PAN * CHUNK // steps, PAN), lambda i: (i, 0)),
        out_shape=jax.ShapeDtypeStruct((PAN * CHUNK, PAN), bf16),
        scratch_shapes=[pltpu.VMEM((CHUNK, PAN), f32)],
        compiler_params=pltpu.CompilerParams(vmem_limit_bytes=BIG),
        name="pack",
    )(far, *pieces, *later)


SRC = LEAF + 2 * RIM
BATCH = 4
FEAT = 48
ORDERS = ((0, 0), (0, 1), (1, 0), (0, 2), (1, 1), (2, 0))


def three(x):
    a = x.astype(bf16).astype(f32)
    b = (x - a).astype(bf16).astype(f32)
    c = (x - a - b).astype(bf16).astype(f32)
    return a, b, c


def near_kernel(index, count, cen, nrm, dens, x1, x3, cross, out, raw, fsrc, ftar, fs, dpar, dwide, ft, sums, dist):
    place = lax.axis_index("sub")
    last = lax.axis_size("sub") - 1
    for q in range(10):
        far_side = cross[4 * q : 4 * q + 4, :]
        at = 16 + 4 * q
        raw[q, 0:RIM, :] = jnp.where(place == 0, far_side, x1[at : at + RIM, :PAN])
        raw[q, RIM + LEAF : SRC, :] = jnp.where(place == last, far_side, x3[at : at + RIM, :PAN])
        if q < 3:
            body = cen[q]
        elif q < 6:
            body = nrm[q - 3]
        else:
            body = dens[LEAF * (q - 6) : LEAF * (q - 5), :]
        raw[q, RIM : RIM + LEAF, :] = body
    xs = [raw[a] - 0.5 for a in range(3)]
    ns = [raw[3 + a] for a in range(3)]
    xt = [cen[a] - 0.5 for a in range(3)]
    xs3 = [three(v) for v in xs]
    ns3 = [three(v) for v in ns]
    xt3 = [three(v) for v in xt]
    ss = three(xs[0] * xs[0] + xs[1] * xs[1] + xs[2] * xs[2] + EPS)
    sn = three(xs[0] * ns[0] + xs[1] * ns[1] + xs[2] * ns[2])
    tt = three(xt[0] * xt[0] + xt[1] * xt[1] + xt[2] * xt[2])
    one_s = jnp.ones((SRC, PAN), f32)
    zero_s = jnp.zeros((SRC, PAN), f32)
    one = jnp.ones((LEAF, PAN), f32)
    zero = jnp.zeros((LEAF, PAN), f32)
    feats = []
    for a in range(3):
        for i, j in ORDERS:
            feats.append((xs3[a][i], -2.0 * xt3[a][j], zero))
            feats.append((ns3[a][i], zero, xt3[a][j]))
    for i in range(3):
        feats.append((ss[i], one, zero))
        feats.append((sn[i], zero, -one))
        feats.append((one_s, tt[i], zero))
    while len(feats) < FEAT:
        feats.append((zero_s, zero, zero))
    for k, (s, t1, t2) in enumerate(feats):
        fsrc[k * SRC : (k + 1) * SRC, :] = s
        ftar[0, k * LEAF : (k + 1) * LEAF, :] = t1
        ftar[1, k * LEAF : (k + 1) * LEAF, :] = t2
    for m in range(SRC):
        fs[m] = fsrc[pl.ds(m, FEAT, stride=SRC), :].T.astype(bf16)
    dcols = iota((16, RHS * PAN), 1) // PAN
    pick_r = (iota((16, RHS * PAN), 0) // 3 == dcols).astype(f32).astype(bf16)
    for r in range(RHS):
        for j, part in enumerate(three(raw[6 + r])):
            dpar[pl.ds(3 * r + j, SRC, stride=16), :] = part
            dpar[pl.ds(12 + j, SRC, stride=16), :] = zero_s
    dpar[pl.ds(15, SRC, stride=16), :] = zero_s
    for m in range(SRC):
        wide = nn(dpar[16 * m : 16 * m + 16, :].T.astype(bf16), pick_r)
        for r in range(RHS):
            dwide[m, r] = wide[:, PAN * r : PAN * (r + 1)]
    dwide[SRC] = jnp.zeros((RHS, PAN, PAN), f32)
    for n in range(LEAF):
        ft[n] = jnp.concatenate(
            [ftar[0, pl.ds(n, FEAT, stride=LEAF), :], ftar[1, pl.ds(n, FEAT, stride=LEAF), :]], 1
        ).astype(bf16)
    sums[...] = jnp.zeros_like(sums)
    dist[:, :, :PAN] = jnp.ones((BATCH, 2 * PAN, PAN), f32)
    dist[:, :, PAN:] = jnp.zeros((BATCH, 2 * PAN, PAN), f32)
    pairs = 0
    for n in range(LEAF):
        pairs = pairs + (count[n] + 1) // 2
    steps = (pairs + BATCH - 1) // BATCH + 1

    def step(_, carry):
        n, i = carry[0], carry[1]
        old = carry[2:]
        for u in range(BATCH):
            n1, p1, q1 = old[3 * u], old[3 * u + 1], old[3 * u + 2]
            inv = lax.rsqrt(dist[u, :, :PAN])
            k = dist[u, :, PAN:] * (inv * inv * inv)
            for r in range(RHS):
                term = k[:PAN] * dwide[p1, r] + k[PAN:] * dwide[q1, r]
                sums[n1, r] += jnp.sum(term.reshape(PAN // 8, 8, PAN), 0)
        fresh = []
        for u in range(BATCH):
            at = jnp.minimum(n, LEAF - 1)
            first = 2 * i
            live1 = n < LEAF
            live2 = live1 & (first + 1 < count[at])
            p = index[at, first]
            q = index[at, jnp.minimum(first + 1, index.shape[1] - 1)]
            dist[u] = nn(jnp.concatenate([fs[p], fs[q]], 0), ft[at])
            fresh += [at, jnp.where(live1, p, SRC), jnp.where(live2, q, SRC)]
            more = live1 & (first + 2 < count[at])
            n = jnp.where(more, n, n + 1)
            i = jnp.where(more, i + 1, 0)
        return (n, i) + tuple(fresh)

    start = [jnp.int32(0), jnp.int32(0)] + [jnp.int32(0), jnp.int32(SRC), jnp.int32(SRC)] * BATCH
    lax.fori_loop(0, steps, step, tuple(start))
    for r in range(RHS):
        out[LEAF * r : LEAF * (r + 1), :] = jnp.sum(sums[:, r], 1)


def near(index, count, cen, nrm, dens, x1, x3, cross):
    outs = jax.ShapeDtypeStruct((ROWS, PAN), f32)
    return pl.pallas_call(
        near_kernel,
        grid=(1,),
        in_specs=[SM, SM] + [whole(x) for x in (cen, nrm, dens, x1, x3, cross)],
        out_specs=whole(outs),
        out_shape=outs,
        scratch_shapes=[
            pltpu.VMEM((10, SRC, PAN), f32),
            pltpu.VMEM((FEAT * SRC, PAN), f32),
            pltpu.VMEM((2, FEAT * LEAF, PAN), f32),
            pltpu.VMEM((SRC, PAN, FEAT), bf16),
            pltpu.VMEM((SRC * 16, PAN), f32),
            pltpu.VMEM((SRC + 1, RHS, PAN, PAN), f32),
            pltpu.VMEM((LEAF, FEAT, 2 * PAN), bf16),
            pltpu.VMEM((LEAF, RHS, 8, PAN), f32),
            pltpu.VMEM((BATCH, 2 * PAN, 2 * PAN), f32),
        ],
        compiler_params=pltpu.CompilerParams(vmem_limit_bytes=BIG),
        cost_estimate=pl.CostEstimate(
            flops=20_000_000_00, bytes_accessed=1_000_000, transcendentals=3_600_000
        ),
        name="near",
    )(index, count, cen, nrm, dens, x1, x3, cross)


def finish_kernel(
    par, octs, far_count, top_count, far_slot, far_op, top_src, top_op, arrived, ops0, ops1, l2l_hbm, tp_hbm, near_part, out,
    ids, slots, kinds, turned, picked, s0, s1, s2, m0, m1, m2, m3, m4, m5, acc, l2l, tp, sems,
):
    step = pl.program_id(0)
    spread = (s0, s1, s2)
    late = (
        pltpu.make_async_copy(l2l_hbm, l2l, sems.at[0]),
        pltpu.make_async_copy(tp_hbm, tp, sems.at[1]),
    )
    even = (m0, m1, m2)
    odd = (m3, m4, m5)
    tail = ops0.shape[2] - 2 * PAN

    @pl.when(step == 0)
    def _():
        for copy in late:
            copy.start()
        acc[...] = jnp.zeros_like(acc)
        m2[...] = jnp.zeros_like(m2)
        m5[...] = jnp.zeros_like(m5)
        for p in range(PAN):
            s0[PITCH * p : PITCH * p + CHUNK, :] = arrived[CHUNK * p : CHUNK * (p + 1), :].astype(f32)
        for j in range(6):
            for t in range(PIECES):
                piece = s0[pl.ds(PIECES * j + t, PAN, stride=PITCH), :].T
                turned[PAN * t : PAN * (t + 1), PAN * j : PAN * (j + 1)] = piece.astype(bf16)

        row = iota((LEAF, far_slot.shape[1]), 0)
        lane = iota((LEAF, far_slot.shape[1]), 1)
        live = jnp.zeros(row.shape, i32)
        for n in range(LEAF):
            live = jnp.where(row == n, far_count[n], live)
        slot = far_slot[...]
        ids[...] = jnp.where(lane < live, (slot % 2) * PAN + slot // 2, -1)
        slots[0:4, :] = jnp.concatenate([ids[pl.ds(h, 4, stride=4), :] for h in range(4)], 1)
        kinds[0:4, :] = jnp.concatenate(
            [far_op[pl.ds(h, 4, stride=4), :] + OPSP * (h % 2) for h in range(4)], 1
        )
        row = iota((LEAF, top_src.shape[1]), 0)
        lane = iota((LEAF, top_src.shape[1]), 1)
        live = jnp.zeros(row.shape, i32)
        for n in range(LEAF):
            live = jnp.where(row == n, top_count[n], live)
        slot = top_src[...]
        ids[:, : row.shape[1]] = jnp.where(lane < live, (slot % 4) * PAN + slot // 4, -1)
        slots[4:6, :] = jnp.concatenate(
            [ids[pl.ds(h, 2, stride=8), :][:, : row.shape[1]] for h in range(8)], 1
        )
        kinds[4:6, :] = jnp.concatenate(
            [top_op[pl.ds(h, 2, stride=8), :] + OPSP * (h % 4) for h in range(8)], 1
        )
        far_row = iota((2 * PAN, 2 * PAN), 0)
        top_row = iota((4 * PAN, 2 * PAN), 0)
        for g in range(6):
            if g < 4:
                hot = (far_row == slots[g : g + 1, :]).astype(f32).astype(bf16)
                table = turned[: RHS * EQ, : 2 * PAN]
            else:
                hot = (top_row == slots[g : g + 1, :]).astype(f32).astype(bf16)
                table = turned[: RHS * EQ, 2 * PAN :]
            picked[g] = nn(table, hot).astype(bf16)

        def build(g, half, per, base):
            ids = kinds[pl.ds(g, 1), :][:, PAN * half : PAN * (half + 1)]
            kind = jnp.broadcast_to(ids, (PAN, PAN)).T
            src = picked[g, :, PAN * half : PAN * (half + 1)]
            for h in range(0, per, 2):
                hot = jnp.concatenate(
                    [
                        (kind == iota((PAN, PAN), 1) + (PAN * t + h * OPSP)).astype(f32).astype(bf16)
                        for t in range(6)
                    ],
                    1,
                )
                y = nn(src, hot)
                for r in range(RHS):
                    for u in range(2):
                        at = pl.multiple_of((base + r * LEAF + h + u) * EQ, 8)
                        for t in range(3):
                            spread[t][pl.ds(at, EQ), :] = y[
                                r * EQ : (r + 1) * EQ, PAN * (t + 3 * u) : PAN * (t + 3 * u + 1)
                            ]

        def far_group(g, carry):
            build(g, 0, 2, g * 4)
            build(g, 1, 2, g * 4 + 2)
            return carry

        def top_group(g, carry):
            build(g, 0, 4, ROWS + (g - 4) * 8)
            build(g, 1, 4, ROWS + (g - 4) * 8 + 4)
            return carry

        lax.fori_loop(0, 4, far_group, 0)
        lax.fori_loop(4, 6, top_group, 0)

    def move(to):
        for h, ops in enumerate((ops0, ops1)):
            rows = ops.shape[0] * 8
            for g in range(FB // 8):
                at = slice(g * 8 * EQ + h * rows, g * 8 * EQ + (h + 1) * rows)
                part = ops[:, 8 * g : 8 * g + 8, :].astype(f32).reshape(rows, ops.shape[2])
                for t in range(2):
                    to[t][at, :] = part[:, PAN * t : PAN * (t + 1)]
                to[2][at, :tail] = part[:, 2 * PAN :]

    def multiply(width, of):
        base = (step - 1) * FB
        left = []
        right = []
        for i in range(width):
            for t in range(3):
                left.append(spread[t][pl.ds(base + i, 2 * ROWS, stride=EQ), :].astype(bf16))
                right.append(of[t][pl.ds(i // 8 * 8 * EQ + i % 8, EQ, stride=8), :].astype(bf16))
        acc[...] += nt(jnp.concatenate(right, 1), jnp.concatenate(left, 1))

    last = pl.num_programs(0) - 1

    @pl.when(step == 0)
    def _():
        move(even)

    @pl.when((step > 0) & (step < last) & (step % 2 == 1))
    def _():
        multiply(FB, even)
        move(odd)

    @pl.when((step > 0) & (step < last) & (step % 2 == 0))
    def _():
        multiply(FB, odd)
        move(even)

    @pl.when(step == last)
    def _():
        multiply(EQ % FB, odd)
        for copy in late:
            copy.wait()
        res = acc[...].T
        far = res[:ROWS]
        top = res[ROWS:].astype(bf16)
        row = iota((ROWS, ROWS), 0)
        lane = iota((ROWS, ROWS), 1)
        parent = jnp.zeros((ROWS, ROWS), i32)
        for n in range(LEAF):
            parent = jnp.where(row % LEAF == n, par[0, n], parent)
        hit = (parent == lane % LEAF) & (row // LEAF == lane // LEAF)
        chosen = nn(hit.astype(f32).astype(bf16), top).astype(bf16)
        leaf_row = iota((ROWS, EQ), 0) % LEAF
        down = jnp.zeros((ROWS, EQ), f32)
        for n in range(LEAF):
            down = jnp.where(leaf_row == n, nt(chosen, l2l[octs[0, n]]), down)
        local = (down + far).astype(bf16)
        leaf_row = iota((ROWS, PAN), 0) % LEAF
        res = jnp.zeros((ROWS, PAN), f32)
        for n in range(LEAF):
            res = jnp.where(leaf_row == n, nn(local, tp[n]), res)
        out[...] = res + near_part[...]


def finish(par, octs, far_count, top_count, far_slot, far_op, top_src, top_op, arrived, tables, l2l, tp, near_part):
    chunks = pl.cdiv(EQ, FB)
    half = (EQ // 2, FB, tables.shape[2])
    return pl.pallas_call(
        finish_kernel,
        grid=(chunks + 1,),
        in_specs=[
            SM,
            SM,
            SM,
            SM,
            whole(far_slot),
            whole(far_op),
            whole(top_src),
            whole(top_op),
            whole(arrived),
            pl.BlockSpec(half, lambda i: (0, jnp.minimum(i, chunks - 1), 0)),
            pl.BlockSpec(half, lambda i: (1, jnp.minimum(i, chunks - 1), 0)),
            pl.BlockSpec(memory_space=pl.ANY),
            pl.BlockSpec(memory_space=pl.ANY),
            whole(near_part),
        ],
        out_specs=pl.BlockSpec((ROWS, PAN), lambda i: (0, 0)),
        out_shape=jax.ShapeDtypeStruct((ROWS, PAN), f32),
        scratch_shapes=[
            pltpu.VMEM((LEAF, 64), i32),
            pltpu.VMEM((8, 2 * PAN), i32),
            pltpu.VMEM((8, 2 * PAN), i32),
            pltpu.VMEM((BOX, 6 * PAN), bf16),
            pltpu.VMEM((6, RHS * EQ, 2 * PAN), bf16),
            pltpu.VMEM((2 * ROWS * EQ, PAN), f32),
            pltpu.VMEM((2 * ROWS * EQ, PAN), f32),
            pltpu.VMEM((2 * ROWS * EQ, PAN), f32),
            pltpu.VMEM((EQ * FB, PAN), f32),
            pltpu.VMEM((EQ * FB, PAN), f32),
            pltpu.VMEM((EQ * FB, PAN), f32),
            pltpu.VMEM((EQ * FB, PAN), f32),
            pltpu.VMEM((EQ * FB, PAN), f32),
            pltpu.VMEM((EQ * FB, PAN), f32),
            pltpu.VMEM((EQ, 2 * ROWS), f32),
            pltpu.VMEM(l2l.shape, bf16),
            pltpu.VMEM(tp.shape, bf16),
            pltpu.SemaphoreType.DMA((2,)),
        ],
        compiler_params=pltpu.CompilerParams(vmem_limit_bytes=BIG),
        name="finish",
    )(par, octs, far_count, top_count, far_slot, far_op, top_src, top_op, arrived, tables, tables, l2l, tp, near_part)


def per_device(
    density,
    centres,
    normal,
    to_multipole,
    to_panels,
    m2m_ops,
    l2l_ops,
    m2l_ops,
    near_index,
    near_count,
    send_box,
    send_count,
    far_slot,
    far_op,
    far_count,
    parent_of,
    octant,
    top_src,
    top_op,
    top_count,
):
    dens = density.reshape(ROWS, PAN)
    mult, own, *others, cross = upward(
        parent_of, octant, dens, centres, normal, to_multipole, m2m_ops
    )
    axes = ("leaf", "sub")
    subs = lax.axis_size("sub")
    count = lax.axis_size("leaf") * subs
    pieces = [own]
    for s, piece in enumerate(others, 1):
        pieces.append(lax.ppermute(piece, "sub", [(i, (i + s) % subs) for i in range(subs)]))
    ends = range(subs - 1, count - 1, subs)
    cross = lax.ppermute(cross, axes, [(i, i + 1) for i in ends] + [(i + 1, i) for i in ends])

    chosen = choose(jnp.transpose(send_box[0]), send_count, mult)
    outgoing = pack(chosen, pieces, (cross,))
    arrived = lax.all_to_all(
        outgoing.reshape(count, CHUNK, PAN), axes, split_axis=0, concat_axis=0, tiled=True
    )

    near_part = near(near_index, near_count, centres, normal, dens, pieces[1], pieces[3], cross)

    res = finish(
        parent_of,
        octant,
        far_count,
        top_count,
        far_slot,
        far_op,
        top_src,
        top_op,
        arrived.reshape(count * CHUNK, PAN),
        jnp.transpose(m2l_ops, (1, 2, 0)),
        l2l_ops,
        jnp.transpose(to_panels, (0, 2, 1)),
        near_part,
    )
    return res.reshape(RHS, LEAF, PAN)


def solution(mesh):
    both = ("leaf", "sub")
    return jax.shard_map(
        per_device,
        mesh=mesh,
        in_specs=(
            P(None, both, None),
            P(None, both, None),
            P(None, both, None),
            P(both, None, None),
            P(both, None, None),
            P(),
            P(),
            P(),
            P(both, None),
            P(both),
            P(both, None, None),
            P(both, None),
            P(both, None),
            P(both, None),
            P(both),
            P("leaf", "sub"),
            P("leaf", "sub"),
            P("leaf", None),
            P("leaf", None),
            P("leaf"),
        ),
        out_specs=P(None, both, None),
        check_vma=False,
    )
```

```python
import jax
import jax.numpy as jnp
from jax import lax
from jax.experimental import pallas as pl
from jax.experimental.pallas import tpu as pltpu
from jax.sharding import PartitionSpec as P

f32 = jnp.float32
bf16 = jnp.bfloat16
i32 = jnp.int32

RIM = 4
LEAF = 16
RHS = 4
ROWS = RHS * LEAF
EQ = 152
OPSP = 384
PAN = 128
BOX = 640
PIECES = 5
CHUNK = 32
PITCH = 40
EPS = 0.01
FB = 16
MIB = 1 << 20
BIG = 64 * MIB

SM = pl.BlockSpec(memory_space=pltpu.SMEM)


def nt(a, b, **kw):
    return lax.dot_general(a, b, (((1,), (1,)), ((), ())), preferred_element_type=f32, **kw)


def nn(a, b, **kw):
    return lax.dot_general(a, b, (((1,), (0,)), ((), ())), preferred_element_type=f32, **kw)


def whole(x):
    return pl.BlockSpec(x.shape, lambda i: (0,) * len(x.shape))


def iota(shape, dim):
    return lax.broadcasted_iota(i32, shape, dim)


def upward_kernel(par, octs, dens, cen, nrm, tm, m2m, mult_out, c0, x1, c2, x3, cross):
    d = dens[...].astype(bf16)
    leaf_row = iota((ROWS, EQ), 0) % LEAF
    mult = jnp.zeros((ROWS, EQ), f32)
    for n in range(LEAF):
        mult = jnp.where(leaf_row == n, nt(d, tm[n]), mult)
    mb = mult.astype(bf16)
    mult_out[...] = mb
    child = jnp.zeros((ROWS, EQ), f32)
    for n in range(LEAF):
        child = jnp.where(leaf_row == n, nt(mb, m2m[octs[0, n]]), child)
    row = iota((ROWS, ROWS), 0)
    lane = iota((ROWS, ROWS), 1)
    parent = jnp.zeros((ROWS, ROWS), i32)
    for n in range(LEAF):
        parent = jnp.where(lane % LEAF == n, par[0, n], parent)
    box = ((row // 16 + lax.axis_index("sub")) % 4) * 4 + row % 4
    hit = (parent == box) & ((row // 4) % 4 == lane // LEAF)
    part = nn(hit.astype(f32), child, precision=lax.Precision.HIGHEST)
    for s, piece in enumerate((c0, x1, c2, x3)):
        piece[:16, :] = part[16 * s : 16 * s + 16]
    first = lax.axis_index("sub") == 0

    def rim(at, ends, starts):
        x1[16 + at : 16 + at + RIM, :PAN] = ends
        x3[16 + at : 16 + at + RIM, :PAN] = starts
        cross[at : at + RIM, :] = jnp.where(first, starts, ends)

    for a in range(3):
        rim(RIM * a, cen[a, LEAF - RIM :, :], cen[a, :RIM, :])
        rim(RIM * (3 + a), nrm[a, LEAF - RIM :, :], nrm[a, :RIM, :])
    for r in range(RHS):
        rim(
            RIM * (6 + r),
            dens[LEAF * (r + 1) - RIM : LEAF * (r + 1), :],
            dens[LEAF * r : LEAF * r + RIM, :],
        )
    for x in (x1, x3):
        x[16:, PAN:] = jnp.zeros((40, EQ - PAN), f32)


def upward(par, octs, dens, cen, nrm, tm, m2m):
    outs = [
        jax.ShapeDtypeStruct((ROWS, EQ), bf16),
    ]
    small = jax.ShapeDtypeStruct((16, EQ), f32)
    large = jax.ShapeDtypeStruct((56, EQ), f32)
    outs += [small, large, small, large, jax.ShapeDtypeStruct((40, PAN), f32)]
    return pl.pallas_call(
        upward_kernel,
        grid=(1,),
        in_specs=[SM, SM] + [whole(x) for x in (dens, cen, nrm, tm, m2m)],
        out_specs=[whole(x) for x in outs],
        out_shape=outs,
        compiler_params=pltpu.CompilerParams(vmem_limit_bytes=BIG),
        name="upward",
    )(par, octs, dens, cen, nrm, tm, m2m)


def pack_kernel(boxes, counts, mult, c0, x1, c2, x3, cross, out, far, const):
    row = iota((EQ, BOX), 0)
    lane = iota((EQ, BOX), 1)
    own = (c0[...] + x1[:16, :]) + (c2[...] + x3[:16, :])
    own = own.astype(bf16).astype(f32)
    mf = mult[...].astype(f32)
    table = jnp.zeros((24, BOX), f32)
    for r in range(RHS):
        both = jnp.concatenate(
            [mf[16 * r : 16 * r + 16], own[4 * r : 4 * r + 4], jnp.zeros((4, EQ), f32)], 0
        )
        place = (lane == row + EQ * r).astype(f32).astype(bf16)
        table = table + nn(both.astype(bf16), place)
    leaf = iota((LEAF, PAN), 0)
    for j in range(2):
        hot = ((boxes[j : j + 1, :] == leaf) & (counts[...] > j)).astype(f32).T
        y = nn(hot.astype(bf16), table[:LEAF].astype(bf16))
        for t in range(PIECES):
            far[pl.ds(PIECES * j + t, PAN, stride=24), :] = y[:, PAN * t : PAN * (t + 1)]
    const[...] = jnp.zeros_like(const)
    for q in range(4):
        for t in range(PIECES):
            at = PIECES * (2 + q) + t
            const[at : at + 1, :] = table[LEAF + q : LEAF + q + 1, PAN * t : PAN * (t + 1)]
    head = const[:16]
    rest = const[16:].astype(bf16)
    is_far = iota((16, PAN), 0) < 2 * PIECES
    for d in range(PAN):
        out[CHUNK * d : CHUNK * d + 16, :] = jnp.where(
            is_far, far[24 * d : 24 * d + 16, :], head
        ).astype(bf16)
        out[CHUNK * d + 16 : CHUNK * (d + 1), :] = rest


def pack(boxes, counts, mult, pieces, later):
    outs = jax.ShapeDtypeStruct((PAN * CHUNK, PAN), bf16)
    return pl.pallas_call(
        pack_kernel,
        grid=(1,),
        in_specs=[whole(x) for x in (boxes, counts, mult, *pieces)]
        + [pl.BlockSpec(memory_space=pl.ANY)] * len(later),
        out_specs=whole(outs),
        out_shape=outs,
        scratch_shapes=[pltpu.VMEM((PAN * 24, PAN), f32), pltpu.VMEM((CHUNK, PAN), f32)],
        compiler_params=pltpu.CompilerParams(vmem_limit_bytes=BIG),
        name="pack",
    )(boxes, counts, mult, *pieces, *later)


SRC = LEAF + 2 * RIM
BATCH = 3
FEAT = 48
ORDERS = ((0, 0), (0, 1), (1, 0), (0, 2), (1, 1), (2, 0))


def three(x):
    a = x.astype(bf16).astype(f32)
    b = (x - a).astype(bf16).astype(f32)
    c = (x - a - b).astype(bf16).astype(f32)
    return a, b, c


def near_kernel(index, count, cen, nrm, dens, x1, x3, cross, out, raw, fsrc, ftar, fs, dpar, dwide, ft, sums, dist):
    place = lax.axis_index("sub")
    last = lax.axis_size("sub") - 1
    for q in range(10):
        far_side = cross[4 * q : 4 * q + 4, :]
        at = 16 + 4 * q
        raw[q, 0:RIM, :] = jnp.where(place == 0, far_side, x1[at : at + RIM, :PAN])
        raw[q, RIM + LEAF : SRC, :] = jnp.where(place == last, far_side, x3[at : at + RIM, :PAN])
        if q < 3:
            body = cen[q]
        elif q < 6:
            body = nrm[q - 3]
        else:
            body = dens[LEAF * (q - 6) : LEAF * (q - 5), :]
        raw[q, RIM : RIM + LEAF, :] = body
    xs = [raw[a] - 0.5 for a in range(3)]
    ns = [raw[3 + a] for a in range(3)]
    xt = [cen[a] - 0.5 for a in range(3)]
    xs3 = [three(v) for v in xs]
    ns3 = [three(v) for v in ns]
    xt3 = [three(v) for v in xt]
    ss = three(xs[0] * xs[0] + xs[1] * xs[1] + xs[2] * xs[2] + EPS)
    sn = three(xs[0] * ns[0] + xs[1] * ns[1] + xs[2] * ns[2])
    tt = three(xt[0] * xt[0] + xt[1] * xt[1] + xt[2] * xt[2])
    one_s = jnp.ones((SRC, PAN), f32)
    zero_s = jnp.zeros((SRC, PAN), f32)
    one = jnp.ones((LEAF, PAN), f32)
    zero = jnp.zeros((LEAF, PAN), f32)
    feats = []
    for a in range(3):
        for i, j in ORDERS:
            feats.append((xs3[a][i], -2.0 * xt3[a][j], zero))
            feats.append((ns3[a][i], zero, xt3[a][j]))
    for i in range(3):
        feats.append((ss[i], one, zero))
        feats.append((sn[i], zero, -one))
        feats.append((one_s, tt[i], zero))
    while len(feats) < FEAT:
        feats.append((zero_s, zero, zero))
    for k, (s, t1, t2) in enumerate(feats):
        fsrc[k * SRC : (k + 1) * SRC, :] = s
        ftar[0, k * LEAF : (k + 1) * LEAF, :] = t1
        ftar[1, k * LEAF : (k + 1) * LEAF, :] = t2
    for m in range(SRC):
        fs[m] = fsrc[pl.ds(m, FEAT, stride=SRC), :].T.astype(bf16)
    dcols = iota((16, RHS * PAN), 1) // PAN
    pick_r = (iota((16, RHS * PAN), 0) // 3 == dcols).astype(f32).astype(bf16)
    for r in range(RHS):
        for j, part in enumerate(three(raw[6 + r])):
            dpar[pl.ds(3 * r + j, SRC, stride=16), :] = part
            dpar[pl.ds(12 + j, SRC, stride=16), :] = zero_s
    dpar[pl.ds(15, SRC, stride=16), :] = zero_s
    for m in range(SRC):
        wide = nn(dpar[16 * m : 16 * m + 16, :].T.astype(bf16), pick_r)
        for r in range(RHS):
            dwide[m, r] = wide[:, PAN * r : PAN * (r + 1)]
    dwide[SRC] = jnp.zeros((RHS, PAN, PAN), f32)
    for n in range(LEAF):
        ft[n] = jnp.concatenate(
            [ftar[0, pl.ds(n, FEAT, stride=LEAF), :], ftar[1, pl.ds(n, FEAT, stride=LEAF), :]], 1
        ).astype(bf16)
    sums[...] = jnp.zeros_like(sums)
    dist[:, :, :PAN] = jnp.ones((BATCH, 2 * PAN, PAN), f32)
    dist[:, :, PAN:] = jnp.zeros((BATCH, 2 * PAN, PAN), f32)
    pairs = 0
    for n in range(LEAF):
        pairs = pairs + (count[n] + 1) // 2
    steps = (pairs + BATCH - 1) // BATCH + 1

    def step(_, carry):
        n, i = carry[0], carry[1]
        old = carry[2:]
        for u in range(BATCH):
            n1, p1, q1 = old[3 * u], old[3 * u + 1], old[3 * u + 2]
            inv = lax.rsqrt(dist[u, :, :PAN])
            k = dist[u, :, PAN:] * (inv * inv * inv)
            for r in range(RHS):
                term = k[:PAN] * dwide[p1, r] + k[PAN:] * dwide[q1, r]
                sums[n1, r] += jnp.sum(term.reshape(PAN // 8, 8, PAN), 0)
        fresh = []
        for u in range(BATCH):
            at = jnp.minimum(n, LEAF - 1)
            first = 2 * i
            live1 = n < LEAF
            live2 = live1 & (first + 1 < count[at])
            p = index[at, first]
            q = index[at, jnp.minimum(first + 1, index.shape[1] - 1)]
            dist[u] = nn(jnp.concatenate([fs[p], fs[q]], 0), ft[at])
            fresh += [at, jnp.where(live1, p, SRC), jnp.where(live2, q, SRC)]
            more = live1 & (first + 2 < count[at])
            n = jnp.where(more, n, n + 1)
            i = jnp.where(more, i + 1, 0)
        return (n, i) + tuple(fresh)

    start = [jnp.int32(0), jnp.int32(0)] + [jnp.int32(0), jnp.int32(SRC), jnp.int32(SRC)] * BATCH
    lax.fori_loop(0, steps, step, tuple(start))
    for r in range(RHS):
        out[LEAF * r : LEAF * (r + 1), :] = jnp.sum(sums[:, r], 1)


def near(index, count, cen, nrm, dens, x1, x3, cross):
    outs = jax.ShapeDtypeStruct((ROWS, PAN), f32)
    return pl.pallas_call(
        near_kernel,
        grid=(1,),
        in_specs=[SM, SM] + [whole(x) for x in (cen, nrm, dens, x1, x3, cross)],
        out_specs=whole(outs),
        out_shape=outs,
        scratch_shapes=[
            pltpu.VMEM((10, SRC, PAN), f32),
            pltpu.VMEM((FEAT * SRC, PAN), f32),
            pltpu.VMEM((2, FEAT * LEAF, PAN), f32),
            pltpu.VMEM((SRC, PAN, FEAT), bf16),
            pltpu.VMEM((SRC * 16, PAN), f32),
            pltpu.VMEM((SRC + 1, RHS, PAN, PAN), f32),
            pltpu.VMEM((LEAF, FEAT, 2 * PAN), bf16),
            pltpu.VMEM((LEAF, RHS, 8, PAN), f32),
            pltpu.VMEM((BATCH, 2 * PAN, 2 * PAN), f32),
        ],
        compiler_params=pltpu.CompilerParams(vmem_limit_bytes=BIG),
        cost_estimate=pl.CostEstimate(
            flops=20_000_000_00, bytes_accessed=1_000_000, transcendentals=3_600_000
        ),
        name="near",
    )(index, count, cen, nrm, dens, x1, x3, cross)


def finish_kernel(
    par, octs, far_count, top_count, far_slot, far_op, top_src, top_op, arrived, ops0, ops1, l2l_hbm, tp_hbm, near_part, out,
    ids, slots, kinds, turned, picked, s0, s1, s2, m0, m1, m2, m3, m4, m5, acc, l2l, tp, sems,
):
    step = pl.program_id(0)
    spread = (s0, s1, s2)
    late = (
        pltpu.make_async_copy(l2l_hbm, l2l, sems.at[0]),
        pltpu.make_async_copy(tp_hbm, tp, sems.at[1]),
    )
    even = (m0, m1, m2)
    odd = (m3, m4, m5)
    tail = ops0.shape[2] - 2 * PAN

    @pl.when(step == 0)
    def _():
        for copy in late:
            copy.start()
        acc[...] = jnp.zeros_like(acc)
        m2[...] = jnp.zeros_like(m2)
        m5[...] = jnp.zeros_like(m5)
        for p in range(PAN):
            s0[PITCH * p : PITCH * p + CHUNK, :] = arrived[CHUNK * p : CHUNK * (p + 1), :].astype(f32)
        for j in range(6):
            for t in range(PIECES):
                piece = s0[pl.ds(PIECES * j + t, PAN, stride=PITCH), :].T
                turned[PAN * t : PAN * (t + 1), PAN * j : PAN * (j + 1)] = piece.astype(bf16)

        row = iota((LEAF, far_slot.shape[1]), 0)
        lane = iota((LEAF, far_slot.shape[1]), 1)
        live = jnp.zeros(row.shape, i32)
        for n in range(LEAF):
            live = jnp.where(row == n, far_count[n], live)
        slot = far_slot[...]
        ids[...] = jnp.where(lane < live, (slot % 2) * PAN + slot // 2, -1)
        slots[0:4, :] = jnp.concatenate([ids[pl.ds(h, 4, stride=4), :] for h in range(4)], 1)
        kinds[0:4, :] = jnp.concatenate(
            [far_op[pl.ds(h, 4, stride=4), :] + OPSP * (h % 2) for h in range(4)], 1
        )
        row = iota((LEAF, top_src.shape[1]), 0)
        lane = iota((LEAF, top_src.shape[1]), 1)
        live = jnp.zeros(row.shape, i32)
        for n in range(LEAF):
            live = jnp.where(row == n, top_count[n], live)
        slot = top_src[...]
        ids[:, : row.shape[1]] = jnp.where(lane < live, (slot % 4) * PAN + slot // 4, -1)
        slots[4:6, :] = jnp.concatenate(
            [ids[pl.ds(h, 2, stride=8), :][:, : row.shape[1]] for h in range(8)], 1
        )
        kinds[4:6, :] = jnp.concatenate(
            [top_op[pl.ds(h, 2, stride=8), :] + OPSP * (h % 4) for h in range(8)], 1
        )
        far_row = iota((2 * PAN, 2 * PAN), 0)
        top_row = iota((4 * PAN, 2 * PAN), 0)
        for g in range(6):
            if g < 4:
                hot = (far_row == slots[g : g + 1, :]).astype(f32).astype(bf16)
                table = turned[: RHS * EQ, : 2 * PAN]
            else:
                hot = (top_row == slots[g : g + 1, :]).astype(f32).astype(bf16)
                table = turned[: RHS * EQ, 2 * PAN :]
            picked[g] = nn(table, hot).astype(bf16)

        def build(g, half, per, base):
            ids = kinds[pl.ds(g, 1), :][:, PAN * half : PAN * (half + 1)]
            kind = jnp.broadcast_to(ids, (PAN, PAN)).T
            src = picked[g, :, PAN * half : PAN * (half + 1)]
            for h in range(0, per, 2):
                hot = jnp.concatenate(
                    [
                        (kind == iota((PAN, PAN), 1) + (PAN * t + h * OPSP)).astype(f32).astype(bf16)
                        for t in range(6)
                    ],
                    1,
                )
                y = nn(src, hot)
                for r in range(RHS):
                    for u in range(2):
                        at = pl.multiple_of((base + r * LEAF + h + u) * EQ, 8)
                        for t in range(3):
                            spread[t][pl.ds(at, EQ), :] = y[
                                r * EQ : (r + 1) * EQ, PAN * (t + 3 * u) : PAN * (t + 3 * u + 1)
                            ]

        def far_group(g, carry):
            build(g, 0, 2, g * 4)
            build(g, 1, 2, g * 4 + 2)
            return carry

        def top_group(g, carry):
            build(g, 0, 4, ROWS + (g - 4) * 8)
            build(g, 1, 4, ROWS + (g - 4) * 8 + 4)
            return carry

        lax.fori_loop(0, 4, far_group, 0)
        lax.fori_loop(4, 6, top_group, 0)

    def move(to):
        for h, ops in enumerate((ops0, ops1)):
            rows = ops.shape[0] * 8
            for g in range(FB // 8):
                at = slice(g * 8 * EQ + h * rows, g * 8 * EQ + (h + 1) * rows)
                part = ops[:, 8 * g : 8 * g + 8, :].astype(f32).reshape(rows, ops.shape[2])
                for t in range(2):
                    to[t][at, :] = part[:, PAN * t : PAN * (t + 1)]
                to[2][at, :tail] = part[:, 2 * PAN :]

    def multiply(width, of):
        base = (step - 1) * FB
        left = []
        right = []
        for i in range(width):
            for t in range(3):
                left.append(spread[t][pl.ds(base + i, 2 * ROWS, stride=EQ), :].astype(bf16))
                right.append(of[t][pl.ds(i // 8 * 8 * EQ + i % 8, EQ, stride=8), :].astype(bf16))
        acc[...] += nt(jnp.concatenate(right, 1), jnp.concatenate(left, 1))

    last = pl.num_programs(0) - 1

    @pl.when(step == 0)
    def _():
        move(even)

    @pl.when((step > 0) & (step < last) & (step % 2 == 1))
    def _():
        multiply(FB, even)
        move(odd)

    @pl.when((step > 0) & (step < last) & (step % 2 == 0))
    def _():
        multiply(FB, odd)
        move(even)

    @pl.when(step == last)
    def _():
        multiply(EQ % FB, odd)
        for copy in late:
            copy.wait()
        res = acc[...].T
        far = res[:ROWS]
        top = res[ROWS:].astype(bf16)
        row = iota((ROWS, ROWS), 0)
        lane = iota((ROWS, ROWS), 1)
        parent = jnp.zeros((ROWS, ROWS), i32)
        for n in range(LEAF):
            parent = jnp.where(row % LEAF == n, par[0, n], parent)
        hit = (parent == lane % LEAF) & (row // LEAF == lane // LEAF)
        chosen = nn(hit.astype(f32).astype(bf16), top).astype(bf16)
        leaf_row = iota((ROWS, EQ), 0) % LEAF
        down = jnp.zeros((ROWS, EQ), f32)
        for n in range(LEAF):
            down = jnp.where(leaf_row == n, nt(chosen, l2l[octs[0, n]]), down)
        local = (down + far).astype(bf16)
        leaf_row = iota((ROWS, PAN), 0) % LEAF
        res = jnp.zeros((ROWS, PAN), f32)
        for n in range(LEAF):
            res = jnp.where(leaf_row == n, nn(local, tp[n]), res)
        out[...] = res + near_part[...]


def finish(par, octs, far_count, top_count, far_slot, far_op, top_src, top_op, arrived, tables, l2l, tp, near_part):
    chunks = pl.cdiv(EQ, FB)
    half = (EQ // 2, FB, tables.shape[2])
    return pl.pallas_call(
        finish_kernel,
        grid=(chunks + 1,),
        in_specs=[
            SM,
            SM,
            SM,
            SM,
            whole(far_slot),
            whole(far_op),
            whole(top_src),
            whole(top_op),
            whole(arrived),
            pl.BlockSpec(half, lambda i: (0, jnp.minimum(i, chunks - 1), 0)),
            pl.BlockSpec(half, lambda i: (1, jnp.minimum(i, chunks - 1), 0)),
            pl.BlockSpec(memory_space=pl.ANY),
            pl.BlockSpec(memory_space=pl.ANY),
            whole(near_part),
        ],
        out_specs=pl.BlockSpec((ROWS, PAN), lambda i: (0, 0)),
        out_shape=jax.ShapeDtypeStruct((ROWS, PAN), f32),
        scratch_shapes=[
            pltpu.VMEM((LEAF, 64), i32),
            pltpu.VMEM((8, 2 * PAN), i32),
            pltpu.VMEM((8, 2 * PAN), i32),
            pltpu.VMEM((BOX, 6 * PAN), bf16),
            pltpu.VMEM((6, RHS * EQ, 2 * PAN), bf16),
            pltpu.VMEM((2 * ROWS * EQ, PAN), f32),
            pltpu.VMEM((2 * ROWS * EQ, PAN), f32),
            pltpu.VMEM((2 * ROWS * EQ, PAN), f32),
            pltpu.VMEM((EQ * FB, PAN), f32),
            pltpu.VMEM((EQ * FB, PAN), f32),
            pltpu.VMEM((EQ * FB, PAN), f32),
            pltpu.VMEM((EQ * FB, PAN), f32),
            pltpu.VMEM((EQ * FB, PAN), f32),
            pltpu.VMEM((EQ * FB, PAN), f32),
            pltpu.VMEM((EQ, 2 * ROWS), f32),
            pltpu.VMEM(l2l.shape, bf16),
            pltpu.VMEM(tp.shape, bf16),
            pltpu.SemaphoreType.DMA((2,)),
        ],
        compiler_params=pltpu.CompilerParams(vmem_limit_bytes=BIG),
        name="finish",
    )(par, octs, far_count, top_count, far_slot, far_op, top_src, top_op, arrived, tables, tables, l2l, tp, near_part)


def per_device(
    density,
    centres,
    normal,
    to_multipole,
    to_panels,
    m2m_ops,
    l2l_ops,
    m2l_ops,
    near_index,
    near_count,
    send_box,
    send_count,
    far_slot,
    far_op,
    far_count,
    parent_of,
    octant,
    top_src,
    top_op,
    top_count,
):
    dens = density.reshape(ROWS, PAN)
    mult, own, *others, cross = upward(
        parent_of, octant, dens, centres, normal, to_multipole, m2m_ops
    )
    axes = ("leaf", "sub")
    subs = lax.axis_size("sub")
    count = lax.axis_size("leaf") * subs
    pieces = [own]
    for s, piece in enumerate(others, 1):
        pieces.append(lax.ppermute(piece, "sub", [(i, (i + s) % subs) for i in range(subs)]))
    ends = range(subs - 1, count - 1, subs)
    cross = lax.ppermute(cross, axes, [(i, i + 1) for i in ends] + [(i + 1, i) for i in ends])

    outgoing = pack(jnp.transpose(send_box[0]), send_count, mult, pieces, (cross,))
    arrived = lax.all_to_all(
        outgoing.reshape(count, CHUNK, PAN), axes, split_axis=0, concat_axis=0, tiled=True
    )

    near_part = near(near_index, near_count, centres, normal, dens, pieces[1], pieces[3], cross)

    res = finish(
        parent_of,
        octant,
        far_count,
        top_count,
        far_slot,
        far_op,
        top_src,
        top_op,
        arrived.reshape(count * CHUNK, PAN),
        jnp.transpose(m2l_ops, (1, 2, 0)),
        l2l_ops,
        jnp.transpose(to_panels, (0, 2, 1)),
        near_part,
    )
    return res.reshape(RHS, LEAF, PAN)


def solution(mesh):
    both = ("leaf", "sub")
    return jax.shard_map(
        per_device,
        mesh=mesh,
        in_specs=(
            P(None, both, None),
            P(None, both, None),
            P(None, both, None),
            P(both, None, None),
            P(both, None, None),
            P(),
            P(),
            P(),
            P(both, None),
            P(both),
            P(both, None, None),
            P(both, None),
            P(both, None),
            P(both, None),
            P(both),
            P("leaf", "sub"),
            P("leaf", "sub"),
            P("leaf", None),
            P("leaf", None),
            P("leaf"),
        ),
        out_specs=P(None, both, None),
        check_vma=False,
    )
```
